512 devices in a mesh: ctx: 64 (over y, x, core), head: 8 (over z).
Axes of the slice: x: 4, y: 8, z: 8, core: 2. Of those that a mesh axis runs over, the one named last changes fastest.
Arguments:
- query_proj: bfloat16 [16384, 3072], P('ctx', 'head'), may hold values from -150 to 150
- key_proj: bfloat16 [16384, 3072], P('ctx', 'head'), may hold values from -150 to 150
- value: bfloat16 [16384, 3072], P('ctx', 'head'), may hold values from -6 to 6
- out_grad: bfloat16 [16384, 3072], P('ctx', 'head'), may hold values from -6 to 6
- query_gain: float32 [3072], P('head'), may hold values from 0.5 to 1.5
- key_gain: float32 [3072], P('head'), may hold values from 0.5 to 1.5
- band_bias: float32 [7, 24], P(None, 'head'), may hold values from -1.5 to 1.5
- tile_mask: int32 [128, 7, 2], P('ctx'), may hold values from 0 to 1, as said below
Outputs:
- attended: bfloat16 [16384, 3072], P('ctx', 'head')
- query_grad: bfloat16 [16384, 3072], P('ctx', 'head')
- key_grad: bfloat16 [16384, 3072], P('ctx', 'head')
- value_grad: bfloat16 [16384, 3072], P('ctx', 'head')
The draws below stay inside these ranges and needn't reach their ends.
Inputs may be any that keep to these rules, and one draw needn't show every extreme that they name: Every entry of band 0 is 1. For b >= 1 the mask is symmetric between the two slabs of a band: tile_mask[i * 2 + r, b, t] equals tile_mask[j * 2 + t, b, r] where j = i XOR 2 ** (b - 1). Farther bands hold fewer live tiles.
All inputs are finite; a program needn't handle non-finite values.
Results may differ from the reference program's by a relative error of at most 0.03.
Values may be sent and summed in bfloat16 or wider, within the bound.
A program may use at most 64 MiB of HBM per device.

```python
import jax
import jax.numpy as jnp
from jax import lax

HD = 128
HEADS = 24
TILE = 128
TOK_DEV = 256
TOKENS = 16384
TPD = 2
TILES = 128
BANDS = 6
N_CTX = 64


def column_scales(key, rising):
    spread = 10.0 ** jax.random.uniform(key, (HEADS * HD,))
    head_ids = (jnp.arange(HEADS * HD) // HD).astype(jnp.float32)
    return spread * rising ** (head_ids / max(HEADS - 1, 1))


def projection(key, rising):
    key_rows, key_vals, key_cols = jax.random.split(key, 3)
    row_scale = 10.0 ** jax.random.uniform(key_rows, (TOKENS, 1))
    normal_vals = jnp.clip(jax.random.normal(key_vals, (TOKENS, HEADS * HD)), -4.0, 4.0)
    return normal_vals * column_scales(key_cols, rising) * row_scale / 10.0


def draw_query_proj(key, part):
    own_key = jax.random.fold_in(key, 11)
    values = projection(own_key, 2.0)
    return values.astype(jnp.bfloat16)


def draw_key_proj(key, part):
    own_key = jax.random.fold_in(key, 12)
    values = projection(own_key, 2.0)
    return values.astype(jnp.bfloat16)


def draw_tile_mask(key, part):
    key = jax.random.fold_in(key, 21)
    raw = jax.random.randint(key, (N_CTX, BANDS + 1, TPD, TPD), 0, 1000)
    band_ids = jnp.arange(BANDS + 1)
    slab_ids = jnp.arange(N_CTX)[:, None]
    shift = jnp.where(band_ids > 0, jnp.left_shift(1, jnp.maximum(band_ids - 1, 0)), 0)
    partners = jnp.bitwise_xor(slab_ids, shift[None, :])
    mirrored = jnp.swapaxes(raw[partners, band_ids[None, :]], 2, 3)
    chosen = jnp.where((slab_ids < partners)[:, :, None, None], raw, mirrored)
    cut = jnp.where(band_ids > 0, 1000 - 600 * band_ids // BANDS, 1000)
    live = (chosen < cut[None, :, None, None]) | (band_ids == 0)[None, :, None, None]
    live = live.astype(jnp.int32).transpose(0, 2, 1, 3)
    return live.reshape(TILES, BANDS + 1, TPD)


def levels(key, dims, cuts, smallest, high):
    level = 1.0
    for dim, shards_of in cuts:
        steps = jax.random.uniform(jax.random.fold_in(jax.random.fold_in(key, 6), dim), (shards_of,), jnp.float32, smallest / len(cuts), high / len(cuts))
        level = level * jnp.repeat(jnp.exp(steps), dims[dim] // shards_of).reshape((-1,) + (1,) * (len(dims) - 1 - dim))
    return level


def centred(key, dims, width, limit, cuts=(), held_as=jnp.bfloat16):
    array = width * jax.random.normal(key, dims, jnp.float32)
    if cuts:
        array = array * levels(key, dims, cuts, -0.22, 0.18)
    return jnp.clip(array, -limit, limit).astype(held_as)


def setup_inputs(seed: int = 0) -> dict:
    keys = jax.random.split(jax.random.key(seed), 9)
    query_proj = draw_query_proj(jax.random.fold_in(keys[8], 71), 0)
    key_proj = draw_key_proj(jax.random.fold_in(keys[8], 71), 0)
    value = centred(keys[2], (TOKENS, HEADS * HD), 1.0, 6.0, ((0, 64), (1, 8)))
    out_grad = centred(keys[3], (TOKENS, HEADS * HD), 1.0, 6.0, ((0, 64), (1, 8)))
    query_gain = jnp.clip(1.0 + 0.1 * jax.random.normal(keys[4], (HEADS * HD,), jnp.float32), 0.5, 1.5)
    key_gain = jnp.clip(1.0 + 0.1 * jax.random.normal(keys[5], (HEADS * HD,), jnp.float32), 0.5, 1.5)
    band_bias = jnp.clip(jax.random.uniform(keys[6], (BANDS + 1, HEADS), jnp.float32, -1.5, 1.5) * levels(keys[6], (BANDS + 1, HEADS), ((1, 8),), -0.4, 0.0), -1.5, 1.5)
    tile_mask = draw_tile_mask(jax.random.fold_in(keys[8], 71), 0)
    return dict(query_proj=query_proj, key_proj=key_proj, value=value, out_grad=out_grad, query_gain=query_gain, key_gain=key_gain, band_bias=band_bias, tile_mask=tile_mask)


epsilon = 1e-06
neg_fill = -1e+30

def expand(tiles):
    return jnp.repeat(jnp.repeat(tiles, TILE, axis=0), TILE, axis=1) > 0

def heads_of(matrix):
    return matrix.reshape(matrix.shape[0], HEADS, HD).astype(jnp.float32)

def slab_of(matrix, index):
    return lax.dynamic_slice_in_dim(matrix, (index * TOK_DEV).astype(jnp.int32), TOK_DEV, 0)

def rounded(values):
    return lax.optimization_barrier(values.astype(jnp.bfloat16)).astype(jnp.float32)

def normalize(matrix, gain):
    values = matrix.astype(jnp.float32)
    factor = lax.rsqrt(lax.optimization_barrier(jnp.sum(values * values, axis=1, keepdims=True)) / (HEADS * HD) + epsilon)
    return ((values * factor * gain.astype(jnp.float32)).astype(jnp.bfloat16), factor)

def norm_back(matrix, factor, gain, grad):
    values = matrix.astype(jnp.float32)
    scaled = gain.astype(jnp.float32) * grad
    inner = lax.optimization_barrier(jnp.sum(scaled * values, axis=1, keepdims=True)) / (HEADS * HD)
    return (factor * scaled - values * factor ** 3 * inner).astype(jnp.bfloat16)

def scores_of(query_heads, key_heads, shift):
    return jnp.einsum('qhd,khd->hqk', query_heads, key_heads) * HD ** (-0.5) + shift[:, None, None]

def pair_grads(query_heads, key_heads, value_heads, grad_heads, log_norm, row_delta, live_mask, shift):
    scores = scores_of(query_heads, key_heads, shift)
    probs = rounded(jnp.where(live_mask, jnp.exp(scores - log_norm[:, :, None]), 0.0))
    value_part = jnp.einsum('hqk,qhd->khd', probs, grad_heads)
    prob_grad = jnp.einsum('qhd,khd->hqk', grad_heads, value_heads)
    score_grad = rounded(probs * (prob_grad - row_delta[:, :, None]))
    query_part = jnp.einsum('hqk,khd->qhd', score_grad, key_heads)
    key_part = jnp.einsum('hqk,qhd->khd', score_grad, query_heads)
    return (query_part, key_part, value_part)

def partner(slab_index, band):
    if band == 0:
        return slab_index
    return jnp.bitwise_xor(slab_index, jnp.int32(1 << band - 1)).astype(jnp.int32)

def reference(query_proj, key_proj, value, out_grad, query_gain, key_gain, band_bias, tile_mask):
    score_scale = HD ** (-0.5)
    query_n, query_factor = normalize(query_proj, query_gain)
    key_n, key_factor = normalize(key_proj, key_gain)
    shifts = band_bias.astype(jnp.float32)

    def live_of(slab_index, band):
        tiles = lax.dynamic_slice_in_dim(tile_mask, (slab_index * TPD).astype(jnp.int32), TPD, 0)[:, band, :]
        return expand(tiles)[None]

    def forward(slab_index):
        query_heads = heads_of(slab_of(query_n, slab_index))
        masked = []
        value_list = []
        for band in range(BANDS + 1):
            other = partner(slab_index, band)
            scores = scores_of(query_heads, heads_of(slab_of(key_n, other)), shifts[band])
            masked.append(jnp.where(live_of(slab_index, band), scores, neg_fill))
            value_list.append(heads_of(slab_of(value, other)))
        row_top = masked[0].max(axis=2)
        for scores in masked[1:]:
            row_top = jnp.maximum(row_top, scores.max(axis=2))
        row_total = jnp.zeros_like(row_top)
        for scores in masked:
            row_total = row_total + jnp.exp(scores - row_top[:, :, None]).sum(axis=2)
        log_norm = row_top + jnp.log(row_total)
        output = jnp.zeros((TOK_DEV, HEADS, HD), jnp.float32)
        for scores, value_heads in zip(masked, value_list):
            output = output + jnp.einsum('hqk,khd->qhd', rounded(jnp.exp(scores - log_norm[:, :, None])), value_heads)
        return (output.reshape(TOK_DEV, HEADS * HD).astype(jnp.bfloat16), log_norm)
    slab_ids = jnp.arange(N_CTX, dtype=jnp.int32)
    outputs, norms = lax.map(forward, slab_ids)
    attended = outputs.reshape(TOKENS, HEADS * HD)
    deltas = lax.optimization_barrier(jnp.sum(heads_of(out_grad) * heads_of(attended), axis=2))
    deltas = deltas.reshape(N_CTX, TOK_DEV, HEADS).transpose(0, 2, 1)

    def backward(slab_index):
        query_heads = heads_of(slab_of(query_n, slab_index))
        key_heads = heads_of(slab_of(key_n, slab_index))
        value_heads = heads_of(slab_of(value, slab_index))
        grad_heads = heads_of(slab_of(out_grad, slab_index))
        own_norm = norms[slab_index]
        own_delta = deltas[slab_index]
        query_acc, key_acc, value_acc = pair_grads(query_heads, key_heads, value_heads, grad_heads, own_norm, own_delta, live_of(slab_index, 0), shifts[0])
        for band in range(1, BANDS + 1):
            other = partner(slab_index, band)
            query_part = pair_grads(query_heads, heads_of(slab_of(key_n, other)), heads_of(slab_of(value, other)), grad_heads, own_norm, own_delta, live_of(slab_index, band), shifts[band])[0]
            query_acc = query_acc + query_part
            unused, key_part, value_part = pair_grads(heads_of(slab_of(query_n, other)), key_heads, value_heads, heads_of(slab_of(out_grad, other)), norms[other], deltas[other], live_of(other, band), shifts[band])
            key_acc = key_acc + key_part
            value_acc = value_acc + value_part
        query_ngrad = (query_acc * score_scale).reshape(TOK_DEV, HEADS * HD)
        key_ngrad = (key_acc * score_scale).reshape(TOK_DEV, HEADS * HD)
        query_grad = norm_back(slab_of(query_proj, slab_index), slab_of(query_factor, slab_index), query_gain, query_ngrad)
        key_grad = norm_back(slab_of(key_proj, slab_index), slab_of(key_factor, slab_index), key_gain, key_ngrad)
        return (query_grad, key_grad, value_acc.reshape(TOK_DEV, HEADS * HD).astype(jnp.bfloat16))
    query_grads, key_grads, value_grads = lax.map(backward, slab_ids)
    return (attended, query_grads.reshape(TOKENS, HEADS * HD), key_grads.reshape(TOKENS, HEADS * HD), value_grads.reshape(TOKENS, HEADS * HD))
```

```python
import functools
import math

import jax
import jax.numpy as jnp
from jax import lax
from jax.experimental import pallas as pl
from jax.experimental.pallas import tpu as pltpu
from jax.sharding import PartitionSpec as P

HD = 128
TILE = 128
BANDS = 7
EPS = 1e-06
NEG = -1e30
LOG2E = math.log2(math.e)
MESH = pl.DeviceIdType.MESH
F32 = jnp.float32
BF16 = jnp.bfloat16


def dot_nt(a, b, precision=None):
    return lax.dot_general(
        a, b, (((1,), (1,)), ((), ())), preferred_element_type=F32, precision=precision
    )


def dot_nn(a, b):
    return lax.dot_general(a, b, (((1,), (0,)), ((), ())), preferred_element_type=F32)


def columns_of(row, lanes=128):
    return jnp.broadcast_to(row, (lanes, row.shape[1])).T


def kernel(
    width,
    query_hbm,
    key_hbm,
    value_hbm,
    grad_hbm,
    query_gain,
    key_gain,
    bias,
    mask,
    att_out,
    dq_out,
    dk_out,
    dv_out,
    slab,
    fact,
    stat,
    zbuf,
    qt,
    kt,
    colq,
    colk,
    sbuf,
    pbuf,
    mrun,
    acc,
    dq,
    dk,
    dv,
    stage,
    load_sem,
    store_sem,
    send_sem,
    recv_sem,
    fact_send,
    fact_recv,
    stat_send,
    stat_recv,
    z_send,
    z_recv,
):
    heads = 3
    scale = HD**-0.5
    ctx = lax.axis_index("ctx")
    z = lax.axis_index("head")
    core = lax.rem(ctx, 2)
    x = lax.rem(ctx // 2, 4)
    y = ctx // 8
    tx = 1 - 2 * lax.rem(x, 2)
    t = 1 - 2 * lax.rem(y, 2)
    s = 1 - 2 * lax.rem(y // 2, 2)
    turns = s != t

    def dev(xn, yn, cn=core):
        return ((lax.rem(yn + 16, 8) * 4 + lax.rem(xn + 8, 4)) * 2 + cn, z)

    p_core = dev(x, y, 1 - core)
    p_x1 = dev(x + tx, y)
    p_xm = dev(x - tx, y)
    p_x2 = dev(x + 2, y)
    p_y1 = dev(x, y + t)
    p_ym = dev(x, y - t)
    p_ys = dev(x, y + s)
    p_y2 = dev(x, y + 2 * s)
    p_ym2 = dev(x, y - 2 * s)
    p_y4 = dev(x, y + 4)
    partners = [p_core, p_x1, p_x2, p_y1, p_y2, p_y4]
    z_peers = [(ctx, lax.rem(z + d, 8)) for d in range(1, 8)]

    hbm = [key_hbm, value_hbm, query_hbm, grad_hbm]

    def load(n):
        if n < 6:
            array, h = n % 2, n // 2
        else:
            array, h = 2 + n % 2, (n - 6) // 2
        return pltpu.make_async_copy(
            hbm[array].at[:, pl.ds(h * HD, HD)], slab.at[0, n], load_sem.at[n]
        )

    for n in (0, 1, 6, 2, 8, 4, 10, 3, 5, 7, 9, 11):
        load(n).start()

    barrier = pltpu.get_barrier_semaphore()
    peers = [p_core, p_x1, p_xm, p_x2, p_y1, p_ym, p_y2, p_ym2, p_y4] + z_peers
    for peer in peers:
        pl.semaphore_signal(barrier, inc=1, device_id=peer, device_id_type=MESH)
    pl.semaphore_wait(barrier, len(peers))

    def move(src, dst, n, way, to):
        return pltpu.make_async_remote_copy(
            src_ref=slab.at[src, n],
            dst_ref=slab.at[dst, n],
            send_sem=send_sem.at[way],
            recv_sem=recv_sem.at[dst, n],
            device_id=to,
            device_id_type=MESH,
        )

    def arrived(dst, n):
        move(0, dst, n, 0, p_core).wait_recv()

    def send_own(n):
        move(0, 4, n, 3, p_y1).start()

        @pl.when(turns)
        def _():
            move(0, 5, n, 4, p_y2).start()

        move(0, 2, n, 1, p_x1).start()
        move(0, 1, n, 0, p_core).start()

    def relay(n):
        arrived(4, n)

        @pl.when(turns)
        def _():
            move(4, 5, n, 5, p_ys).start()

        arrived(2, n)
        move(2, 3, n, 2, p_xm).start()

    def relay_far(n):
        arrived(5, n)
        move(5, 6, n, 6, p_ym2).start()

    def z_move(phase, d):
        return pltpu.make_async_remote_copy(
            src_ref=zbuf.at[phase, 0],
            dst_ref=zbuf.at[phase, d],
            send_sem=z_send.at[phase, d],
            recv_sem=z_recv.at[phase, d],
            device_id=z_peers[d - 1],
            device_id_type=MESH,
        )

    def z_sum(phase):
        total = zbuf[phase, 0]
        for d in range(1, 8):
            z_move(phase, d).wait_recv()
            total = total + zbuf[phase, d]
        return total

    def small_move(buf, send, recv, band):
        return pltpu.make_async_remote_copy(
            src_ref=buf.at[0],
            dst_ref=buf.at[band],
            send_sem=send.at[band],
            recv_sem=recv.at[band],
            device_id=partners[band - 1],
            device_id_type=MESH,
        )

    fact_move = functools.partial(small_move, fact, fact_send, fact_recv)
    stat_move = functools.partial(small_move, stat, stat_send, stat_recv)

    for n in range(6):
        load(n).wait()
        send_own(n)
    for n in range(6, 12):
        load(n).wait()

    ones = jnp.ones((8, HD), F32)
    row_id = lax.broadcasted_iota(jnp.int32, (8, 2 * TILE), 0)

    query_sq = jnp.zeros((8, 2 * TILE), F32)
    key_sq = jnp.zeros((8, 2 * TILE), F32)
    for h in range(heads):
        q_vals = slab[0, 6 + 2 * h].astype(F32)
        k_vals = slab[0, 2 * h].astype(F32)
        query_sq += dot_nt(ones, q_vals * q_vals, lax.Precision.HIGHEST)
        key_sq += dot_nt(ones, k_vals * k_vals, lax.Precision.HIGHEST)
    zbuf[0, 0] = jnp.where(row_id == 0, query_sq, key_sq)
    for d in range(1, 8):
        z_move(0, d).start()
    fact[0] = lax.rsqrt(z_sum(0) / width + EPS)
    for band in range(1, BANDS):
        fact_move(band).start()
    colq[...] = columns_of(fact[0, 0:1, :])
    colk[...] = columns_of(fact[0, 1:2, :])

    def gain_of(h):
        cols = pl.ds(h * HD, HD)
        return (query_gain[cols] * key_gain[cols] * scale)[None, :]

    for h in range(heads):
        both = gain_of(h) * LOG2E
        qt[h] = (slab[0, 6 + 2 * h].astype(F32) * colq[...] * both).astype(BF16)
        kt[h] = (slab[0, 2 * h].astype(F32) * colk[...] * both).astype(BF16)

    def shift_of(b, h, r, c):
        return jnp.where(mask[r, b, c] > 0, bias[b, h] * LOG2E, NEG)

    halves = [slice(0, TILE), slice(TILE, 2 * TILE)]

    def score_bands(h, low, high):
        def body(b, carry):
            factor = fact[b, 1:2, :]
            for r in range(2):
                scores = dot_nt(qt[h, halves[r], :], slab[b, 2 * h])
                top = mrun[halves[r], :]
                for c in range(2):
                    part = scores[:, halves[c]] * factor[:, halves[c]] + shift_of(b, h, r, c)
                    sbuf[b, halves[r], halves[c]] = part
                    top = jnp.maximum(top, part)
                mrun[halves[r], :] = top
            return carry

        lax.fori_loop(low, high, body, 0)

    def forward(h):
        top = jnp.max(mrun[...], axis=1, keepdims=True)
        acc[...] = jnp.zeros_like(acc)

        def exp_band(b, carry):
            for r in range(2):
                total = acc[halves[r], :]
                for c in range(2):
                    e = jnp.exp2(sbuf[b, halves[r], halves[c]] - top[halves[r], :])
                    sbuf[b, halves[r], halves[c]] = e
                    total = total + e
                acc[halves[r], :] = total
            return carry

        lax.fori_loop(0, BANDS, exp_band, 0)
        total = jnp.sum(acc[...], axis=1, keepdims=True)
        inverse = 1.0 / total
        lse = top + jnp.log(total) * LOG2E
        acc[...] = jnp.zeros_like(acc)

        def out_band(b, carry):
            for r in range(2):
                p = (sbuf[b, halves[r], :] * inverse[halves[r], :]).astype(BF16)
                pbuf[b, halves[r], :] = p
                acc[halves[r], :] += dot_nn(p, slab[b, 2 * h + 1])
            return carry

        lax.fori_loop(0, BANDS, out_band, 0)
        att = acc[...].astype(BF16)
        stage[0, h] = att
        store(0, h).start()
        delta = jnp.sum(slab[0, 7 + 2 * h].astype(F32) * att.astype(F32), axis=1, keepdims=True)
        stat[0, h : h + 1, :] = jnp.broadcast_to(lse, (2 * TILE, TILE)).T[0:1, :]
        stat[0, 3 + h : 4 + h, :] = jnp.broadcast_to(delta, (2 * TILE, TILE)).T[0:1, :]
        dq[h] = jnp.zeros_like(acc)

        def grad_band(b, carry):
            factor = fact[b, 1:2, :]
            for r in range(2):
                dp = dot_nt(slab[0, 7 + 2 * h, halves[r], :], slab[b, 2 * h + 1])
                p = pbuf[b, halves[r], :].astype(F32)
                ds = (p * (dp - delta[halves[r], :]) * factor).astype(BF16)
                dq[h, halves[r], :] += dot_nn(ds, slab[b, 2 * h])
            return carry

        lax.fori_loop(0, BANDS, grad_band, 0)

    def key_bands(h, low, high):
        def body(b, carry):
            factor = fact[b, 0:1, :]
            lse = stat[b, h : h + 1, :]
            delta = stat[b, 3 + h : 4 + h, :]
            for r in range(2):
                scores = dot_nt(kt[h, halves[r], :], slab[b, 6 + 2 * h])
                parts = []
                for c in range(2):
                    rest = shift_of(b, h, r, c) - lse[:, halves[c]]
                    parts.append(jnp.exp2(scores[:, halves[c]] * factor[:, halves[c]] + rest))
                p = jnp.concatenate(parts, axis=1)
                dv[h, halves[r], :] += dot_nn(p.astype(BF16), slab[b, 7 + 2 * h])
                dp = dot_nt(slab[0, 2 * h + 1, halves[r], :], slab[b, 7 + 2 * h])
                ds = (p * (dp - delta) * factor).astype(BF16)
                dk[h, halves[r], :] += dot_nn(ds, slab[b, 6 + 2 * h])
            return carry

        lax.fori_loop(low, high, body, 0)

    outs = [att_out, dq_out, dk_out, dv_out]

    def store(which, h):
        return pltpu.make_async_copy(
            stage.at[which, h], outs[which].at[:, pl.ds(h * HD, HD)], store_sem.at[which, h]
        )

    def inner_start(phase, total, base):
        inner = jnp.zeros((8, 2 * TILE), F32)
        for h in range(heads):
            scaled = total[h] * gain_of(h)
            total[h] = scaled
            inner += dot_nt(
                ones, scaled * slab[0, base + 2 * h].astype(F32), lax.Precision.HIGHEST
            )
        zbuf[phase, 0] = inner
        for d in range(1, 8):
            z_move(phase, d).start()

    def inner_finish(phase, total, base, col, which):
        inner = columns_of(z_sum(phase)[0:1, :] / width)
        factor = col[...]
        cubed = factor * factor * factor * inner
        for h in range(heads):
            vals = slab[0, base + 2 * h].astype(F32)
            stage[which, h] = (factor * total[h] - vals * cubed).astype(BF16)
            store(which, h).start()

    def fresh():
        mrun[...] = jnp.full(mrun.shape, NEG, F32)

    def near(n):
        arrived(1, n)
        arrived(3, n)

    dk[...] = jnp.zeros_like(dk)
    dv[...] = jnp.zeros_like(dv)
    for h in range(heads):
        n = 2 * h
        if h == 0:
            relay(0)
            relay(1)
            relay_far(0)
        relay(n + 2)
        relay_far(n + 1)
        send_own(6 + 2 * h)
        if h == 0:
            for band in range(1, BANDS):
                fact_move(band).wait_recv()
        fresh()
        near(n)
        score_bands(h, 0, 6)
        relay(n + 3)
        relay_far(n + 2)
        send_own(7 + 2 * h)
        near(n + 1)
        arrived(6, n)
        score_bands(h, 6, 7)
        arrived(6, n + 1)
        forward(h)
    for band in range(1, BANDS):
        stat_move(band).start()
    inner_start(1, dq, 6)
    for h in range(heads):
        n = 6 + 2 * h
        if n + 2 < 12:
            relay(n + 2)
        relay_far(n + 1)
        if h == 0:
            for band in range(1, BANDS):
                stat_move(band).wait_recv()
        near(n)
        near(n + 1)
        key_bands(h, 0, 6)
        if n + 2 < 12:
            relay(n + 3)
            relay_far(n + 2)
        if h == 0:
            inner_finish(1, dq, 6, colq, 1)
        arrived(6, n)
        arrived(6, n + 1)
        key_bands(h, 6, 7)
        stage[3, h] = dv[h].astype(BF16)
        store(3, h).start()
    inner_start(2, dk, 0)
    inner_finish(2, dk, 0, colk, 2)

    for which in range(4):
        for h in range(heads):
            store(which, h).wait()
    for phase in range(3):
        for d in range(1, 8):
            z_move(phase, d).wait_send()
    for band in range(1, BANDS):
        fact_move(band).wait_send()
        stat_move(band).wait_send()

    def sent(way):
        pltpu.make_async_remote_copy(
            src_ref=slab.at[0],
            dst_ref=slab.at[1],
            send_sem=send_sem.at[way],
            recv_sem=recv_sem.at[1, 0],
            device_id=p_core,
            device_id_type=MESH,
        ).wait_send()

    for way in (0, 1, 2, 3, 6):
        sent(way)

    @pl.when(turns)
    def _():
        sent(4)
        sent(5)


def on_device(query_proj, key_proj, value, out_grad, query_gain, key_gain, band_bias, tile_mask):
    rows, cols = query_proj.shape
    width = cols * lax.axis_size("head")
    hbm = pl.BlockSpec(memory_space=pl.ANY)
    vmem = pl.BlockSpec(memory_space=pltpu.VMEM)
    smem = pl.BlockSpec(memory_space=pltpu.SMEM)
    heads = cols // HD
    return pl.pallas_call(
        functools.partial(kernel, width),
        out_shape=[jax.ShapeDtypeStruct((rows, cols), BF16)] * 4,
        in_specs=[hbm] * 4 + [vmem] * 2 + [smem] * 2,
        out_specs=[hbm] * 4,
        scratch_shapes=[
            pltpu.VMEM((BANDS, 4 * heads, rows, HD), BF16),
            pltpu.VMEM((BANDS, 8, rows), F32),
            pltpu.VMEM((BANDS, 8, rows), F32),
            pltpu.VMEM((3, 8, 8, rows), F32),
            pltpu.VMEM((heads, rows, HD), BF16),
            pltpu.VMEM((heads, rows, HD), BF16),
            pltpu.VMEM((rows, TILE), F32),
            pltpu.VMEM((rows, TILE), F32),
            pltpu.VMEM((BANDS, rows, rows), F32),
            pltpu.VMEM((BANDS, rows, rows), BF16),
            pltpu.VMEM((rows, TILE), F32),
            pltpu.VMEM((rows, TILE), F32),
            pltpu.VMEM((heads, rows, HD), F32),
            pltpu.VMEM((heads, rows, HD), F32),
            pltpu.VMEM((heads, rows, HD), F32),
            pltpu.VMEM((4, heads, rows, HD), BF16),
            pltpu.SemaphoreType.DMA((4 * heads,)),
            pltpu.SemaphoreType.DMA((4, heads)),
            pltpu.SemaphoreType.DMA((7,)),
            pltpu.SemaphoreType.DMA((BANDS, 4 * heads)),
            pltpu.SemaphoreType.DMA((BANDS,)),
            pltpu.SemaphoreType.DMA((BANDS,)),
            pltpu.SemaphoreType.DMA((BANDS,)),
            pltpu.SemaphoreType.DMA((BANDS,)),
            pltpu.SemaphoreType.DMA((3, 8)),
            pltpu.SemaphoreType.DMA((3, 8)),
        ],
        compiler_params=pltpu.CompilerParams(
            collective_id=0, has_side_effects=True, vmem_limit_bytes=40 * 2**20
        ),
    )(query_proj, key_proj, value, out_grad, query_gain, key_gain, band_bias, tile_mask)


def solution(mesh):
    placed = (
        P("ctx", "head"),
        P("ctx", "head"),
        P("ctx", "head"),
        P("ctx", "head"),
        P("head"),
        P("head"),
        P(None, "head"),
        P("ctx", None, None),
    )
    return jax.shard_map(
        on_device,
        mesh=mesh,
        in_specs=placed,
        out_specs=(P("ctx", "head"), P("ctx", "head"), P("ctx", "head"), P("ctx", "head")),
        check_vma=False,
    )
```

```python
import functools
import math

import jax
import jax.numpy as jnp
from jax import lax
from jax.experimental import pallas as pl
from jax.experimental.pallas import tpu as pltpu
from jax.sharding import PartitionSpec as P

HD = 128
TILE = 128
BANDS = 7
WINDOW = 3
EPS = 1e-06
NEG = -1e30
LOG2E = math.log2(math.e)
MESH = pl.DeviceIdType.MESH
F32 = jnp.float32
BF16 = jnp.bfloat16


def dot_nt(a, b, precision=None):
    return lax.dot_general(
        a, b, (((1,), (1,)), ((), ())), preferred_element_type=F32, precision=precision
    )


def dot_nn(a, b):
    return lax.dot_general(a, b, (((1,), (0,)), ((), ())), preferred_element_type=F32)


def columns_of(row, lanes=128):
    return jnp.broadcast_to(row, (lanes, row.shape[1])).T


def kernel(
    width,
    query_hbm,
    key_hbm,
    value_hbm,
    grad_hbm,
    query_gain,
    key_gain,
    bias,
    mask,
    att_out,
    dq_out,
    dk_out,
    dv_out,
    slab,
    fact,
    stat,
    zbuf,
    qt,
    kt,
    colq,
    colk,
    sbuf,
    pbuf,
    mrun,
    acc,
    dq,
    dk,
    dv,
    stage,
    load_sem,
    store_sem,
    send_sem,
    recv_sem,
    fact_send,
    fact_recv,
    stat_send,
    stat_recv,
    z_send,
    z_recv,
):
    heads = 3
    scale = HD**-0.5
    ctx = lax.axis_index("ctx")
    z = lax.axis_index("head")
    core = lax.rem(ctx, 2)
    x = lax.rem(ctx // 2, 4)
    y = ctx // 8
    tx = 1 - 2 * lax.rem(x, 2)
    t = 1 - 2 * lax.rem(y, 2)
    s = 1 - 2 * lax.rem(y // 2, 2)
    turns = s != t

    def dev(xn, yn, cn=core):
        return ((lax.rem(yn + 16, 8) * 4 + lax.rem(xn + 8, 4)) * 2 + cn, z)

    p_core = dev(x, y, 1 - core)
    p_x1 = dev(x + tx, y)
    p_xm = dev(x - tx, y)
    p_x2 = dev(x + 2, y)
    p_y1 = dev(x, y + t)
    p_ym = dev(x, y - t)
    p_ys = dev(x, y + s)
    p_y2 = dev(x, y + 2 * s)
    p_ym2 = dev(x, y - 2 * s)
    p_y4 = dev(x, y + 4)
    partners = [p_core, p_x1, p_x2, p_y1, p_y2, p_y4]
    z_peers = [(ctx, lax.rem(z + d, 8)) for d in range(1, 8)]

    hbm = [key_hbm, value_hbm, query_hbm, grad_hbm]

    def load(n):
        if n < 6:
            array, h = n % 2, n // 2
        else:
            array, h = 2 + n % 2, (n - 6) // 2
        return pltpu.make_async_copy(
            hbm[array].at[:, pl.ds(h * HD, HD)], slab.at[0, n], load_sem.at[n]
        )

    for n in (0, 1, 6, 2, 8, 4, 10, 3, 5, 7, 9, 11):
        load(n).start()

    barrier = pltpu.get_barrier_semaphore()
    peers = [p_core, p_x1, p_xm, p_x2, p_y1, p_ym, p_y2, p_ym2, p_y4] + z_peers
    for peer in peers:
        pl.semaphore_signal(barrier, inc=1, device_id=peer, device_id_type=MESH)
    pl.semaphore_wait(barrier, len(peers))

    def move(src, dst, n, way, to):
        return pltpu.make_async_remote_copy(
            src_ref=slab.at[src, n],
            dst_ref=slab.at[dst, n],
            send_sem=send_sem.at[way],
            recv_sem=recv_sem.at[dst, n],
            device_id=to,
            device_id_type=MESH,
        )

    def arrived(dst, n):
        move(0, dst, n, 0, p_core).wait_recv()

    def send_own(n):
        move(0, 4, n, 3, p_y1).start()

        @pl.when(turns)
        def _():
            move(0, 5, n, 4, p_y2).start()

        move(0, 2, n, 1, p_x1).start()
        move(0, 1, n, 0, p_core).start()

    def relay(n):
        arrived(4, n)

        @pl.when(turns)
        def _():
            move(4, 5, n, 5, p_ys).start()

        arrived(2, n)
        move(2, 3, n, 2, p_xm).start()

    def relay_far(n):
        arrived(5, n)
        move(5, 6, n, 6, p_ym2).start()

    def z_move(phase, d):
        return pltpu.make_async_remote_copy(
            src_ref=zbuf.at[phase, 0],
            dst_ref=zbuf.at[phase, d],
            send_sem=z_send.at[phase, d],
            recv_sem=z_recv.at[phase, d],
            device_id=z_peers[d - 1],
            device_id_type=MESH,
        )

    def z_sum(phase):
        total = zbuf[phase, 0]
        for d in range(1, 8):
            z_move(phase, d).wait_recv()
            total = total + zbuf[phase, d]
        return total

    def small_move(buf, send, recv, band):
        return pltpu.make_async_remote_copy(
            src_ref=buf.at[0],
            dst_ref=buf.at[band],
            send_sem=send.at[band],
            recv_sem=recv.at[band],
            device_id=partners[band - 1],
            device_id_type=MESH,
        )

    fact_move = functools.partial(small_move, fact, fact_send, fact_recv)
    stat_move = functools.partial(small_move, stat, stat_send, stat_recv)

    for n in range(WINDOW):
        load(n).wait()
        send_own(n)
    for n in range(WINDOW, 12):
        load(n).wait()

    ones = jnp.ones((8, HD), F32)
    row_id = lax.broadcasted_iota(jnp.int32, (8, 2 * TILE), 0)

    query_sq = jnp.zeros((8, 2 * TILE), F32)
    key_sq = jnp.zeros((8, 2 * TILE), F32)
    for h in range(heads):
        q_vals = slab[0, 6 + 2 * h].astype(F32)
        k_vals = slab[0, 2 * h].astype(F32)
        query_sq += dot_nt(ones, q_vals * q_vals, lax.Precision.HIGHEST)
        key_sq += dot_nt(ones, k_vals * k_vals, lax.Precision.HIGHEST)
    zbuf[0, 0] = jnp.where(row_id == 0, query_sq, key_sq)
    for d in range(1, 8):
        z_move(0, d).start()
    def gain_of(h):
        cols = pl.ds(h * HD, HD)
        return (query_gain[cols] * key_gain[cols] * scale)[None, :]

    def factors():
        fact[0] = lax.rsqrt(z_sum(0) / width + EPS)
        for band in range(1, BANDS):
            fact_move(band).start()
        colq[...] = columns_of(fact[0, 0:1, :])
        colk[...] = columns_of(fact[0, 1:2, :])
        for h in range(heads):
            both = gain_of(h) * LOG2E
            qt[h] = (slab[0, 6 + 2 * h].astype(F32) * colq[...] * both).astype(BF16)
            kt[h] = (slab[0, 2 * h].astype(F32) * colk[...] * both).astype(BF16)

    def shift_of(b, h, r, c):
        return jnp.where(mask[r, c, b] > 0, bias[h, b] * LOG2E, NEG)

    halves = [slice(0, TILE), slice(TILE, 2 * TILE)]

    def score_bands(h, low, high):
        def body(b, carry):
            factor = fact[b, 1:2, :]
            for r in range(2):
                scores = dot_nt(qt[h, halves[r], :], slab[b, 2 * h])
                top = mrun[halves[r], :]
                for c in range(2):
                    part = scores[:, halves[c]] * factor[:, halves[c]] + shift_of(b, h, r, c)
                    sbuf[b, halves[r], halves[c]] = part
                    top = jnp.maximum(top, part)
                mrun[halves[r], :] = top
            return carry

        lax.fori_loop(low, high, body, 0, unroll=True)

    def forward(h):
        top = jnp.max(mrun[...], axis=1, keepdims=True)
        acc[...] = jnp.zeros_like(acc)

        def exp_band(b, carry):
            for r in range(2):
                total = acc[halves[r], :]
                for c in range(2):
                    e = jnp.exp2(sbuf[b, halves[r], halves[c]] - top[halves[r], :])
                    sbuf[b, halves[r], halves[c]] = e
                    total = total + e
                acc[halves[r], :] = total
            return carry

        lax.fori_loop(0, BANDS, exp_band, 0, unroll=True)
        total = jnp.sum(acc[...], axis=1, keepdims=True)
        inverse = 1.0 / total
        lse = top + jnp.log(total) * LOG2E
        acc[...] = jnp.zeros_like(acc)

        def out_band(b, carry):
            for r in range(2):
                p = (sbuf[b, halves[r], :] * inverse[halves[r], :]).astype(BF16)
                pbuf[b, halves[r], :] = p
                acc[halves[r], :] += dot_nn(p, slab[b, 2 * h + 1])
            return carry

        lax.fori_loop(0, BANDS, out_band, 0, unroll=True)
        att = acc[...].astype(BF16)
        stage[0, h] = att
        store(0, h).start()
        delta = jnp.sum(slab[0, 7 + 2 * h].astype(F32) * att.astype(F32), axis=1, keepdims=True)
        stat[0, h : h + 1, :] = jnp.broadcast_to(lse, (2 * TILE, TILE)).T[0:1, :]
        stat[0, 3 + h : 4 + h, :] = jnp.broadcast_to(delta, (2 * TILE, TILE)).T[0:1, :]
        dq[h] = jnp.zeros_like(acc)

        def grad_band(b, carry):
            factor = fact[b, 1:2, :]
            for r in range(2):
                dp = dot_nt(slab[0, 7 + 2 * h, halves[r], :], slab[b, 2 * h + 1])
                p = pbuf[b, halves[r], :].astype(F32)
                ds = (p * (dp - delta[halves[r], :]) * factor).astype(BF16)
                dq[h, halves[r], :] += dot_nn(ds, slab[b, 2 * h])
            return carry

        lax.fori_loop(0, BANDS, grad_band, 0, unroll=True)

    def key_bands(h, low, high):
        def body(b, carry):
            factor = fact[b, 0:1, :]
            lse = stat[b, h : h + 1, :]
            delta = stat[b, 3 + h : 4 + h, :]
            for r in range(2):
                scores = dot_nt(kt[h, halves[r], :], slab[b, 6 + 2 * h])
                parts = []
                for c in range(2):
                    rest = shift_of(b, h, r, c) - lse[:, halves[c]]
                    parts.append(jnp.exp2(scores[:, halves[c]] * factor[:, halves[c]] + rest))
                p = jnp.concatenate(parts, axis=1)
                dv[h, halves[r], :] += dot_nn(p.astype(BF16), slab[b, 7 + 2 * h])
                dp = dot_nt(slab[0, 2 * h + 1, halves[r], :], slab[b, 7 + 2 * h])
                ds = (p * (dp - delta) * factor).astype(BF16)
                dk[h, halves[r], :] += dot_nn(ds, slab[b, 6 + 2 * h])
            return carry

        lax.fori_loop(low, high, body, 0, unroll=True)

    outs = [att_out, dq_out, dk_out, dv_out]

    def store(which, h):
        return pltpu.make_async_copy(
            stage.at[which, h], outs[which].at[:, pl.ds(h * HD, HD)], store_sem.at[which, h]
        )

    def inner_add(phase, total, base, h):
        scaled = total[h] * gain_of(h)
        total[h] = scaled
        part = dot_nt(ones, scaled * slab[0, base + 2 * h].astype(F32), lax.Precision.HIGHEST)
        if h > 0:
            part += zbuf[phase, 0]
        zbuf[phase, 0] = part

    def inner_start(phase):
        for d in range(1, 8):
            z_move(phase, d).start()

    def inner_finish(phase, total, base, col, which):
        inner = columns_of(z_sum(phase)[0:1, :] / width)
        factor = col[...]
        cubed = factor * factor * factor * inner
        for h in range(heads):
            vals = slab[0, base + 2 * h].astype(F32)
            stage[which, h] = (factor * total[h] - vals * cubed).astype(BF16)
            store(which, h).start()

    dk[...] = jnp.zeros_like(dk)
    dv[...] = jnp.zeros_like(dv)

    def all_here(n):
        for k in (n, n + 1):
            arrived(1, k)
            arrived(3, k)
            arrived(6, k)

    def query_side(h):
        all_here(2 * h)
        mrun[...] = jnp.full(mrun.shape, NEG, F32)
        score_bands(h, 0, BANDS)
        forward(h)
        inner_add(1, dq, 6, h)

    for n in range(12):
        relay(n)
        if n > 0:
            relay_far(n - 1)
        if n + WINDOW < 12:
            send_own(n + WINDOW)
        if n == 1:
            factors()
        if n == 3:
            for band in range(1, BANDS):
                fact_move(band).wait_recv()
        if n in (4, 6, 8):
            query_side(n // 2 - 2)
        if n == 8:
            for band in range(1, BANDS):
                stat_move(band).start()
            inner_start(1)
        if n == 10:
            inner_finish(1, dq, 6, colq, 1)
    relay_far(11)
    for band in range(1, BANDS):
        stat_move(band).wait_recv()
    for h in range(heads):
        n = 6 + 2 * h
        for k in (n, n + 1):
            arrived(1, k)
            arrived(3, k)
        key_bands(h, 0, 6)
        arrived(6, n)
        arrived(6, n + 1)
        key_bands(h, 6, 7)
        inner_add(2, dk, 0, h)
        stage[3, h] = dv[h].astype(BF16)
        store(3, h).start()
    inner_start(2)
    inner_finish(2, dk, 0, colk, 2)

    for which in range(4):
        for h in range(heads):
            store(which, h).wait()
    for phase in range(3):
        for d in range(1, 8):
            z_move(phase, d).wait_send()
    for band in range(1, BANDS):
        fact_move(band).wait_send()
        stat_move(band).wait_send()

    def sent(way):
        pltpu.make_async_remote_copy(
            src_ref=slab.at[0],
            dst_ref=slab.at[1],
            send_sem=send_sem.at[way],
            recv_sem=recv_sem.at[1, 0],
            device_id=p_core,
            device_id_type=MESH,
        ).wait_send()

    for way in (0, 1, 2, 3, 6):
        sent(way)

    @pl.when(turns)
    def _():
        sent(4)
        sent(5)


def hand_over(*refs):
    held, in_sem, out_sem = refs[8:]
    here = [pltpu.make_async_copy(refs[i], held.at[i], in_sem.at[i]) for i in range(4)]
    away = [pltpu.make_async_copy(held.at[i], refs[4 + i], out_sem.at[i]) for i in range(4)]
    for copy in here:
        copy.start()
    for i in range(4):
        here[i].wait()
        away[i].start()
    for copy in away:
        copy.wait()


def on_device(query_proj, key_proj, value, out_grad, query_gain, key_gain, band_bias, tile_mask):
    rows, cols = query_proj.shape
    width = cols * lax.axis_size("head")
    hbm = pl.BlockSpec(memory_space=pl.ANY)
    vmem = pl.BlockSpec(memory_space=pltpu.VMEM)
    smem = pl.BlockSpec(memory_space=pltpu.SMEM)
    heads = cols // HD
    outs = pl.pallas_call(
        functools.partial(kernel, width),
        out_shape=[jax.ShapeDtypeStruct((rows, cols), BF16)] * 4,
        in_specs=[hbm] * 4 + [vmem] * 2 + [smem] * 2,
        out_specs=[hbm] * 4,
        scratch_shapes=[
            pltpu.VMEM((BANDS, 4 * heads, rows, HD), BF16),
            pltpu.VMEM((BANDS, 8, rows), F32),
            pltpu.VMEM((BANDS, 8, rows), F32),
            pltpu.VMEM((3, 8, 8, rows), F32),
            pltpu.VMEM((heads, rows, HD), BF16),
            pltpu.VMEM((heads, rows, HD), BF16),
            pltpu.VMEM((rows, TILE), F32),
            pltpu.VMEM((rows, TILE), F32),
            pltpu.VMEM((BANDS, rows, rows), F32),
            pltpu.VMEM((BANDS, rows, rows), BF16),
            pltpu.VMEM((rows, TILE), F32),
            pltpu.VMEM((rows, TILE), F32),
            pltpu.VMEM((heads, rows, HD), F32),
            pltpu.VMEM((heads, rows, HD), F32),
            pltpu.VMEM((heads, rows, HD), F32),
            pltpu.VMEM((4, heads, rows, HD), BF16),
            pltpu.SemaphoreType.DMA((4 * heads,)),
            pltpu.SemaphoreType.DMA((4, heads)),
            pltpu.SemaphoreType.DMA((7,)),
            pltpu.SemaphoreType.DMA((BANDS, 4 * heads)),
            pltpu.SemaphoreType.DMA((BANDS,)),
            pltpu.SemaphoreType.DMA((BANDS,)),
            pltpu.SemaphoreType.DMA((BANDS,)),
            pltpu.SemaphoreType.DMA((BANDS,)),
            pltpu.SemaphoreType.DMA((3, 8)),
            pltpu.SemaphoreType.DMA((3, 8)),
        ],
        compiler_params=pltpu.CompilerParams(
            collective_id=0, has_side_effects=True, vmem_limit_bytes=60 * 2**20
        ),
    )(
        query_proj,
        key_proj,
        value,
        out_grad,
        query_gain,
        key_gain,
        band_bias.T,
        tile_mask.transpose(0, 2, 1),
    )
    return pl.pallas_call(
        hand_over,
        out_shape=[jax.ShapeDtypeStruct((rows, cols), BF16)] * 4,
        in_specs=[hbm] * 4,
        out_specs=[hbm] * 4,
        scratch_shapes=[
            pltpu.VMEM((4, rows, cols), BF16),
            pltpu.SemaphoreType.DMA((4,)),
            pltpu.SemaphoreType.DMA((4,)),
        ],
        compiler_params=pltpu.CompilerParams(vmem_limit_bytes=60 * 2**20),
    )(*outs)


def solution(mesh):
    placed = (
        P("ctx", "head"),
        P("ctx", "head"),
        P("ctx", "head"),
        P("ctx", "head"),
        P("head"),
        P("head"),
        P(None, "head"),
        P("ctx", None, None),
    )
    return jax.shard_map(
        on_device,
        mesh=mesh,
        in_specs=placed,
        out_specs=(P("ctx", "head"), P("ctx", "head"), P("ctx", "head"), P("ctx", "head")),
        check_vma=False,
    )
```

```python
import functools
import math

import jax
import jax.numpy as jnp
from jax import lax
from jax.experimental import pallas as pl
from jax.experimental.pallas import tpu as pltpu
from jax.sharding import PartitionSpec as P

HD = 128
TILE = 128
BANDS = 7
WINDOW = 2
BACK = 1
EPS = 1e-06
NEG = -1e30
LOG2E = math.log2(math.e)
MESH = pl.DeviceIdType.MESH
F32 = jnp.float32
BF16 = jnp.bfloat16


def dot_nt(a, b, precision=None):
    return lax.dot_general(
        a, b, (((1,), (1,)), ((), ())), preferred_element_type=F32, precision=precision
    )


def dot_nn(a, b):
    return lax.dot_general(a, b, (((1,), (0,)), ((), ())), preferred_element_type=F32)


def dot_tn(a, b):
    return lax.dot_general(a, b, (((0,), (0,)), ((), ())), preferred_element_type=F32)


def columns_of(row, lanes=128):
    return jnp.broadcast_to(row, (lanes, row.shape[1])).T


def kernel(
    width,
    query_hbm,
    key_hbm,
    value_hbm,
    grad_hbm,
    query_gain,
    key_gain,
    bias,
    mask,
    att_out,
    dq_out,
    dk_out,
    dv_out,
    slab,
    fact,
    stat,
    zbuf,
    qt,
    kt,
    colq,
    colk,
    sbuf,
    pbuf,
    mrun,
    acc,
    dq,
    dk,
    dv,
    stage,
    part,
    rin,
    dsb,
    back_send,
    back_recv,
    load_sem,
    store_sem,
    send_sem,
    recv_sem,
    fact_send,
    fact_recv,
    stat_send,
    stat_recv,
    z_send,
    z_recv,
):
    heads = 3
    scale = HD**-0.5
    ctx = lax.axis_index("ctx")
    z = lax.axis_index("head")
    core = lax.rem(ctx, 2)
    x = lax.rem(ctx // 2, 4)
    y = ctx // 8
    tx = 1 - 2 * lax.rem(x, 2)
    t = 1 - 2 * lax.rem(y, 2)
    s = 1 - 2 * lax.rem(y // 2, 2)
    turns = s != t

    def dev(xn, yn, cn=core):
        return ((lax.rem(yn + 16, 8) * 4 + lax.rem(xn + 8, 4)) * 2 + cn, z)

    p_core = dev(x, y, 1 - core)
    p_x1 = dev(x + tx, y)
    p_xm = dev(x - tx, y)
    p_x2 = dev(x + 2, y)
    p_y1 = dev(x, y + t)
    p_ym = dev(x, y - t)
    p_ys = dev(x, y + s)
    p_y2 = dev(x, y + 2 * s)
    p_ym2 = dev(x, y - 2 * s)
    p_y4 = dev(x, y + 4)
    partners = [p_core, p_x1, p_x2, p_y1, p_y2, p_y4]
    z_peers = [(ctx, lax.rem(z + d, 8)) for d in range(1, 8)]

    hbm = [key_hbm, value_hbm, query_hbm, grad_hbm]

    def load(n):
        if n < 6:
            array, h = n % 2, n // 2
        else:
            array, h = 2 + n % 2, (n - 6) // 2
        return pltpu.make_async_copy(
            hbm[array].at[:, pl.ds(h * HD, HD)], slab.at[0, n], load_sem.at[n]
        )

    for n in (0, 1, 6, 2, 8, 4, 10, 3, 5, 7, 9, 11):
        load(n).start()

    barrier = pltpu.get_barrier_semaphore()
    peers = [p_core, p_x1, p_xm, p_x2, p_y1, p_ym, p_y2, p_ym2, p_y4] + z_peers
    for peer in peers:
        pl.semaphore_signal(barrier, inc=1, device_id=peer, device_id_type=MESH)
    pl.semaphore_wait(barrier, len(peers))

    def move(src, dst, n, way, to):
        return pltpu.make_async_remote_copy(
            src_ref=slab.at[src, n],
            dst_ref=slab.at[dst, n],
            send_sem=send_sem.at[way],
            recv_sem=recv_sem.at[dst, n],
            device_id=to,
            device_id_type=MESH,
        )

    def arrived(dst, n):
        move(0, dst, n, 0, p_core).wait_recv()

    main = list(range(6)) + list(range(6 + 2 * BACK, 12))

    def send_side(n):
        move(0, 2, n, 1, p_x1).start()
        move(0, 1, n, 0, p_core).start()

    def send_own(n):
        move(0, 4, n, 3, p_y1).start()

        @pl.when(turns)
        def _():
            move(0, 5, n, 4, p_y2).start()

        send_side(n)

    def relay_side(n):
        arrived(2, n)
        move(2, 3, n, 2, p_xm).start()

    def relay(n):
        arrived(4, n)

        @pl.when(turns)
        def _():
            move(4, 5, n, 5, p_ys).start()

        relay_side(n)

    def back(src, kind, h, to):
        return pltpu.make_async_remote_copy(
            src_ref=part.at[src, h],
            dst_ref=rin.at[kind, h],
            send_sem=back_send.at[src, h],
            recv_sem=back_recv.at[kind, h],
            device_id=to,
            device_id_type=MESH,
        )

    def joined(src, kind, h):
        for c in range(2):
            both = part[src, h, c].astype(F32) + rin[kind, h, c].astype(F32)
            part[src, h, c] = both.astype(BF16)

    def back_first(h):
        back(2, 0, h, p_ym2).start()

        @pl.when(jnp.logical_not(turns))
        def _():
            back(0, 3, h, p_y1).start()

    def back_second(h):
        back(2, 0, h, p_ym2).wait_recv()
        joined(1, 0, h)

        @pl.when(turns)
        def _():
            back(1, 1, h, p_ys).start()

        @pl.when(jnp.logical_not(turns))
        def _():
            back(1, 2, h, p_y2).start()

    def back_third(h):
        @pl.when(turns)
        def _():
            back(1, 1, h, p_ys).wait_recv()
            joined(0, 1, h)
            back(0, 3, h, p_y1).start()

    def back_last(h):
        back(0, 3, h, p_y1).wait_recv()
        dk[h] += rin[3, h, 0].astype(F32)
        dv[h] += rin[3, h, 1].astype(F32)

        @pl.when(turns)
        def _():
            back(1, 2, h, p_y2).wait_recv()
            dk[h] += rin[2, h, 0].astype(F32)
            dv[h] += rin[2, h, 1].astype(F32)

    def relay_far(n):
        arrived(5, n)
        move(5, 6, n, 6, p_ym2).start()

    def z_move(phase, d):
        return pltpu.make_async_remote_copy(
            src_ref=zbuf.at[phase, 0],
            dst_ref=zbuf.at[phase, d],
            send_sem=z_send.at[phase, d],
            recv_sem=z_recv.at[phase, d],
            device_id=z_peers[d - 1],
            device_id_type=MESH,
        )

    def z_sum(phase):
        total = zbuf[phase, 0]
        for d in range(1, 8):
            z_move(phase, d).wait_recv()
            total = total + zbuf[phase, d]
        return total

    def small_move(buf, send, recv, band):
        return pltpu.make_async_remote_copy(
            src_ref=buf.at[0],
            dst_ref=buf.at[band],
            send_sem=send.at[band],
            recv_sem=recv.at[band],
            device_id=partners[band - 1],
            device_id_type=MESH,
        )

    fact_move = functools.partial(small_move, fact, fact_send, fact_recv)
    stat_move = functools.partial(small_move, stat, stat_send, stat_recv)

    for n in range(WINDOW):
        load(n).wait()
        send_own(n)
    for n in range(WINDOW, 12):
        load(n).wait()

    ones = jnp.ones((8, HD), F32)

    query_sq = jnp.zeros((8, 2 * TILE), F32)
    key_sq = jnp.zeros((8, 2 * TILE), F32)
    for h in range(heads):
        q_vals = slab[0, 6 + 2 * h].astype(F32)
        k_vals = slab[0, 2 * h].astype(F32)
        query_sq += dot_nt(ones, q_vals * q_vals, lax.Precision.HIGHEST)
        key_sq += dot_nt(ones, k_vals * k_vals, lax.Precision.HIGHEST)
    zbuf[0, 0, 0:1, :] = query_sq[0:1]
    zbuf[0, 0, 1:2, :] = key_sq[0:1]
    for d in range(1, 8):
        z_move(0, d).start()
    def gain_of(h):
        cols = pl.ds(h * HD, HD)
        return (query_gain[cols] * key_gain[cols] * scale)[None, :]

    def factors():
        fact[0] = lax.rsqrt(z_sum(0) / width + EPS)
        for band in range(1, BANDS):
            fact_move(band).start()
        colq[...] = columns_of(fact[0, 0:1, :])
        colk[...] = columns_of(fact[0, 1:2, :])
        for h in range(heads):
            both = gain_of(h) * LOG2E
            qt[h] = (slab[0, 6 + 2 * h].astype(F32) * colq[...] * both).astype(BF16)
            kt[h] = (slab[0, 2 * h].astype(F32) * colk[...] * both).astype(BF16)

    def shift_of(b, h, r, c):
        return jnp.where(mask[r, c, b] > 0, bias[h, b] * LOG2E, NEG)

    halves = [slice(0, TILE), slice(TILE, 2 * TILE)]

    def score_bands(h, low, high):
        def body(b, carry):
            factor = fact[b, 1:2, :]
            for r in range(2):
                scores = dot_nt(qt[h, halves[r], :], slab[b, 2 * h])
                top = mrun[halves[r], :]
                for c in range(2):
                    part = scores[:, halves[c]] * factor[:, halves[c]] + shift_of(b, h, r, c)
                    sbuf[b, halves[r], halves[c]] = part
                    top = jnp.maximum(top, part)
                mrun[halves[r], :] = top
            return carry

        lax.fori_loop(low, high, body, 0, unroll=True)

    def forward(h):
        top = jnp.max(mrun[...], axis=1, keepdims=True)
        acc[...] = jnp.zeros_like(acc)

        def exp_band(b, carry):
            for r in range(2):
                total = acc[halves[r], :]
                for c in range(2):
                    e = jnp.exp2(sbuf[b, halves[r], halves[c]] - top[halves[r], :])
                    sbuf[b, halves[r], halves[c]] = e
                    total = total + e
                acc[halves[r], :] = total
            return carry

        lax.fori_loop(0, BANDS, exp_band, 0, unroll=True)
        total = jnp.sum(acc[...], axis=1, keepdims=True)
        inverse = 1.0 / total
        lse = top + jnp.log(total) * LOG2E
        acc[...] = jnp.zeros_like(acc)

        def out_band(b, carry):
            for r in range(2):
                p = (sbuf[b, halves[r], :] * inverse[halves[r], :]).astype(BF16)
                pbuf[b, halves[r], :] = p
                acc[halves[r], :] += dot_nn(p, slab[b, 2 * h + 1])
            return carry

        lax.fori_loop(0, BANDS, out_band, 0, unroll=True)
        att = acc[...].astype(BF16)
        stage[0, h] = att
        store(0, h).start()
        delta = jnp.sum(slab[0, 7 + 2 * h].astype(F32) * att.astype(F32), axis=1, keepdims=True)
        stat[0, h : h + 1, :] = jnp.broadcast_to(lse, (2 * TILE, TILE)).T[0:1, :]
        stat[0, 3 + h : 4 + h, :] = jnp.broadcast_to(delta, (2 * TILE, TILE)).T[0:1, :]
        dq[h] = jnp.zeros_like(acc)

        normed = (slab[0, 6 + 2 * h].astype(F32) * colq[...]).astype(BF16)

        def grad_band(b):
            factor = fact[b, 1:2, :]
            send_back = h < BACK and b >= 4
            for r in range(2):
                dp = dot_nt(slab[0, 7 + 2 * h, halves[r], :], slab[b, 2 * h + 1])
                p = pbuf[b, halves[r], :].astype(F32)
                ds = p * (dp - delta[halves[r], :])
                if send_back:
                    dsb[halves[r], :] = ds.astype(BF16)
                dq[h, halves[r], :] += dot_nn((ds * factor).astype(BF16), slab[b, 2 * h])
            if send_back:
                part[b - 4, h, 0] = dot_tn(dsb[...], normed).astype(BF16)
                part[b - 4, h, 1] = dot_tn(pbuf[b], slab[0, 7 + 2 * h]).astype(BF16)

        for b in reversed(range(BANDS)):
            grad_band(b)
            if h < BACK and b == 4:
                back_first(h)

    def key_bands(h, low, high):
        def body(b, carry):
            factor = fact[b, 0:1, :]
            lse = stat[b, h : h + 1, :]
            delta = stat[b, 3 + h : 4 + h, :]
            for r in range(2):
                scores = dot_nt(kt[h, halves[r], :], slab[b, 6 + 2 * h])
                parts = []
                for c in range(2):
                    rest = shift_of(b, h, r, c) - lse[:, halves[c]]
                    parts.append(jnp.exp2(scores[:, halves[c]] * factor[:, halves[c]] + rest))
                p = jnp.concatenate(parts, axis=1)
                dv[h, halves[r], :] += dot_nn(p.astype(BF16), slab[b, 7 + 2 * h])
                dp = dot_nt(slab[0, 2 * h + 1, halves[r], :], slab[b, 7 + 2 * h])
                ds = (p * (dp - delta) * factor).astype(BF16)
                dk[h, halves[r], :] += dot_nn(ds, slab[b, 6 + 2 * h])
            return carry

        lax.fori_loop(low, high, body, 0, unroll=True)

    outs = [att_out, dq_out, dk_out, dv_out]

    def store(which, h):
        return pltpu.make_async_copy(
            stage.at[which, h], outs[which].at[:, pl.ds(h * HD, HD)], store_sem.at[which, h]
        )

    def inner_add(phase, total, base, h):
        scaled = total[h] * gain_of(h)
        total[h] = scaled
        part = dot_nt(ones, scaled * slab[0, base + 2 * h].astype(F32), lax.Precision.HIGHEST)[0:1]
        if h > 0:
            part += zbuf[phase, 0, 0:1, :]
        zbuf[phase, 0, 0:1, :] = part[0:1]

    def inner_start(phase):
        for d in range(1, 8):
            z_move(phase, d).start()

    def inner_finish(phase, total, base, col, which):
        inner = columns_of(z_sum(phase)[0:1, :] / width)
        factor = col[...]
        cubed = factor * factor * factor * inner
        for h in range(heads):
            vals = slab[0, base + 2 * h].astype(F32)
            stage[which, h] = (factor * total[h] - vals * cubed).astype(BF16)
            store(which, h).start()

    dk[...] = jnp.zeros_like(dk)
    zbuf[1, 0] = jnp.zeros((2, 2 * TILE), F32)
    zbuf[2, 0] = jnp.zeros((2, 2 * TILE), F32)
    dv[...] = jnp.zeros_like(dv)

    def all_here(n):
        for k in (n, n + 1):
            arrived(1, k)
            arrived(3, k)
            arrived(6, k)

    def query_side(h):
        all_here(2 * h)
        mrun[...] = jnp.full(mrun.shape, NEG, F32)
        score_bands(h, 0, BANDS)
        forward(h)
        inner_add(1, dq, 6, h)

    sides = list(range(6, 6 + 2 * BACK))
    later = {}
    for h in range(BACK):
        later.setdefault(2 * h + 5, []).append(functools.partial(back_second, h))
        later.setdefault(2 * h + 7, []).append(functools.partial(back_third, h))
    for m in range(len(main)):
        relay(main[m])
        if m > 0:
            relay_far(main[m - 1])
        if m + WINDOW < len(main):
            send_own(main[m + WINDOW])
        if m > 2 and sides:
            relay_side(sides.pop(0))
        if 0 < m <= 2 * BACK:
            send_side(5 + m)
        if m == 1:
            factors()
        if m == 2:
            for band in range(1, BANDS):
                fact_move(band).wait_recv()
        for step in later.pop(m, []):
            step()
        if m in (3, 5, 7):
            query_side((m - 3) // 2)
        if m == 7:
            for band in range(1, BANDS):
                stat_move(band).start()
            inner_start(1)
    relay_far(main[-1])
    for n in sides:
        relay_side(n)
    for m in sorted(later):
        for step in later[m]:
            step()
    inner_finish(1, dq, 6, colq, 1)
    for band in range(1, BANDS):
        stat_move(band).wait_recv()
    for h in range(heads):
        n = 6 + 2 * h
        for k in (n, n + 1):
            arrived(1, k)
            arrived(3, k)
        if h < BACK:
            key_bands(h, 0, 4)
            back_last(h)
        else:
            key_bands(h, 0, 6)
            arrived(6, n)
            arrived(6, n + 1)
            key_bands(h, 6, 7)
        inner_add(2, dk, 0, h)
        stage[3, h] = dv[h].astype(BF16)
        store(3, h).start()
    inner_start(2)
    inner_finish(2, dk, 0, colk, 2)

    for which in range(4):
        for h in range(heads):
            store(which, h).wait()
    for phase in range(3):
        for d in range(1, 8):
            z_move(phase, d).wait_send()
    for band in range(1, BANDS):
        fact_move(band).wait_send()
        stat_move(band).wait_send()

    def sent(way, count):
        pltpu.make_async_remote_copy(
            src_ref=slab.at[0, 0:count],
            dst_ref=slab.at[1, 0:count],
            send_sem=send_sem.at[way],
            recv_sem=recv_sem.at[1, 0],
            device_id=p_core,
            device_id_type=MESH,
        ).wait_send()

    for way in (0, 1, 2):
        sent(way, 12)
    for way in (3, 6):
        sent(way, len(main))

    @pl.when(turns)
    def _():
        sent(4, len(main))
        sent(5, len(main))

    for h in range(BACK):
        for src in range(3):
            back(src, 0, h, p_y1).wait_send()


def hand_over(*refs):
    held, in_sem, out_sem = refs[8:]
    here = [pltpu.make_async_copy(refs[i], held.at[i], in_sem.at[i]) for i in range(4)]
    away = [pltpu.make_async_copy(held.at[i], refs[4 + i], out_sem.at[i]) for i in range(4)]
    for copy in here:
        copy.start()
    for i in range(4):
        here[i].wait()
        away[i].start()
    for copy in away:
        copy.wait()


def on_device(query_proj, key_proj, value, out_grad, query_gain, key_gain, band_bias, tile_mask):
    rows, cols = query_proj.shape
    width = cols * lax.axis_size("head")
    hbm = pl.BlockSpec(memory_space=pl.ANY)
    vmem = pl.BlockSpec(memory_space=pltpu.VMEM)
    smem = pl.BlockSpec(memory_space=pltpu.SMEM)
    heads = cols // HD
    outs = pl.pallas_call(
        functools.partial(kernel, width),
        out_shape=[jax.ShapeDtypeStruct((rows, cols), BF16)] * 4,
        in_specs=[hbm] * 4 + [vmem] * 2 + [smem] * 2,
        out_specs=[hbm] * 4,
        scratch_shapes=[
            pltpu.VMEM((BANDS, 4 * heads, rows, HD), BF16),
            pltpu.VMEM((BANDS, 2, rows), F32),
            pltpu.VMEM((BANDS, 8, rows), F32),
            pltpu.VMEM((3, 8, 2, rows), F32),
            pltpu.VMEM((heads, rows, HD), BF16),
            pltpu.VMEM((heads, rows, HD), BF16),
            pltpu.VMEM((rows, TILE), F32),
            pltpu.VMEM((rows, TILE), F32),
            pltpu.VMEM((BANDS, rows, rows), F32),
            pltpu.VMEM((BANDS, rows, rows), BF16),
            pltpu.VMEM((rows, TILE), F32),
            pltpu.VMEM((rows, TILE), F32),
            pltpu.VMEM((heads, rows, HD), F32),
            pltpu.VMEM((heads, rows, HD), F32),
            pltpu.VMEM((heads, rows, HD), F32),
            pltpu.VMEM((4, heads, rows, HD), BF16),
            pltpu.VMEM((3, BACK, 2, rows, HD), BF16),
            pltpu.VMEM((4, BACK, 2, rows, HD), BF16),
            pltpu.VMEM((rows, rows), BF16),
            pltpu.SemaphoreType.DMA((4, BACK)),
            pltpu.SemaphoreType.DMA((4, BACK)),
            pltpu.SemaphoreType.DMA((4 * heads,)),
            pltpu.SemaphoreType.DMA((4, heads)),
            pltpu.SemaphoreType.DMA((7,)),
            pltpu.SemaphoreType.DMA((BANDS, 4 * heads)),
            pltpu.SemaphoreType.DMA((BANDS,)),
            pltpu.SemaphoreType.DMA((BANDS,)),
            pltpu.SemaphoreType.DMA((BANDS,)),
            pltpu.SemaphoreType.DMA((BANDS,)),
            pltpu.SemaphoreType.DMA((3, 8)),
            pltpu.SemaphoreType.DMA((3, 8)),
        ],
        compiler_params=pltpu.CompilerParams(
            collective_id=0, has_side_effects=True, vmem_limit_bytes=60 * 2**20
        ),
    )(
        query_proj,
        key_proj,
        value,
        out_grad,
        query_gain,
        key_gain,
        band_bias.T,
        tile_mask.transpose(0, 2, 1),
    )
    return pl.pallas_call(
        hand_over,
        out_shape=[jax.ShapeDtypeStruct((rows, cols), BF16)] * 4,
        in_specs=[hbm] * 4,
        out_specs=[hbm] * 4,
        scratch_shapes=[
            pltpu.VMEM((4, rows, cols), BF16),
            pltpu.SemaphoreType.DMA((4,)),
            pltpu.SemaphoreType.DMA((4,)),
        ],
        compiler_params=pltpu.CompilerParams(vmem_limit_bytes=60 * 2**20),
    )(*outs)


def solution(mesh):
    placed = (
        P("ctx", "head"),
        P("ctx", "head"),
        P("ctx", "head"),
        P("ctx", "head"),
        P("head"),
        P("head"),
        P(None, "head"),
        P("ctx", None, None),
    )
    return jax.shard_map(
        on_device,
        mesh=mesh,
        in_specs=placed,
        out_specs=(P("ctx", "head"), P("ctx", "head"), P("ctx", "head"), P("ctx", "head")),
        check_vma=False,
    )
```

```python
import functools
import math

import jax
import jax.numpy as jnp
from jax import lax
from jax.experimental import pallas as pl
from jax.experimental.pallas import tpu as pltpu
from jax.sharding import PartitionSpec as P

HD = 128
TILE = 128
BANDS = 7
WINDOW = 2
BACK = 1
EPS = 1e-06
NEG = -1e30
LOG2E = math.log2(math.e)
MESH = pl.DeviceIdType.MESH
F32 = jnp.float32
BF16 = jnp.bfloat16


def dot_nt(a, b, precision=None):
    return lax.dot_general(
        a, b, (((1,), (1,)), ((), ())), preferred_element_type=F32, precision=precision
    )


def dot_nn(a, b):
    return lax.dot_general(a, b, (((1,), (0,)), ((), ())), preferred_element_type=F32)


def dot_tn(a, b):
    return lax.dot_general(a, b, (((0,), (0,)), ((), ())), preferred_element_type=F32)


def columns_of(row, lanes=128):
    return jnp.broadcast_to(row, (lanes, row.shape[1])).T


def kernel(
    width,
    query_hbm,
    key_hbm,
    value_hbm,
    grad_hbm,
    query_gain,
    key_gain,
    bias,
    mask,
    att_out,
    dq_out,
    dk_out,
    dv_out,
    slab,
    fact,
    stat,
    zbuf,
    qt,
    kt,
    colq,
    colk,
    sbuf,
    pbuf,
    mrun,
    acc,
    dq,
    dk,
    dv,
    stage,
    part,
    rin,
    dsb,
    back_send,
    back_recv,
    load_sem,
    store_sem,
    send_sem,
    recv_sem,
    fact_send,
    fact_recv,
    stat_send,
    stat_recv,
    z_send,
    z_recv,
):
    heads = 3
    scale = HD**-0.5
    ctx = lax.axis_index("ctx")
    z = lax.axis_index("head")
    core = lax.rem(ctx, 2)
    x = lax.rem(ctx // 2, 4)
    y = ctx // 8
    tx = 1 - 2 * lax.rem(x, 2)
    t = 1 - 2 * lax.rem(y, 2)
    s = 1 - 2 * lax.rem(y // 2, 2)
    turns = s != t

    def dev(xn, yn, cn=core):
        return ((lax.rem(yn + 16, 8) * 4 + lax.rem(xn + 8, 4)) * 2 + cn, z)

    p_core = dev(x, y, 1 - core)
    p_x1 = dev(x + tx, y)
    p_xm = dev(x - tx, y)
    p_x2 = dev(x + 2, y)
    p_y1 = dev(x, y + t)
    p_ym = dev(x, y - t)
    p_ys = dev(x, y + s)
    p_y2 = dev(x, y + 2 * s)
    p_ym2 = dev(x, y - 2 * s)
    p_y4 = dev(x, y + 4)
    partners = [p_core, p_x1, p_x2, p_y1, p_y2, p_y4]
    z_peers = [(ctx, lax.rem(z + d, 8)) for d in range(1, 8)]

    hbm = [key_hbm, value_hbm, query_hbm, grad_hbm]

    def load(n):
        if n < 6:
            array, h = n % 2, n // 2
        else:
            array, h = 2 + n % 2, (n - 6) // 2
        return pltpu.make_async_copy(
            hbm[array].at[:, pl.ds(h * HD, HD)], slab.at[0, n], load_sem.at[n]
        )

    for n in (0, 1, 6, 2, 8, 4, 10, 3, 5, 7, 9, 11):
        load(n).start()

    barrier = pltpu.get_barrier_semaphore()
    peers = [p_core, p_x1, p_xm, p_x2, p_y1, p_ym, p_y2, p_ym2, p_y4] + z_peers
    for peer in peers:
        pl.semaphore_signal(barrier, inc=1, device_id=peer, device_id_type=MESH)
    pl.semaphore_wait(barrier, len(peers))

    def move(src, dst, n, way, to):
        return pltpu.make_async_remote_copy(
            src_ref=slab.at[src, n],
            dst_ref=slab.at[dst, n],
            send_sem=send_sem.at[way],
            recv_sem=recv_sem.at[dst, n],
            device_id=to,
            device_id_type=MESH,
        )

    def arrived(dst, n):
        move(0, dst, n, 0, p_core).wait_recv()

    main = list(range(6)) + list(range(6 + 2 * BACK, 12))

    def send_side(n):
        move(0, 2, n, 1, p_x1).start()
        move(0, 1, n, 0, p_core).start()

    def send_own(n):
        move(0, 4, n, 3, p_y1).start()

        @pl.when(turns)
        def _():
            move(0, 5, n, 4, p_y2).start()

        send_side(n)

    def relay_side(n):
        arrived(2, n)
        move(2, 3, n, 2, p_xm).start()

    def relay(n):
        arrived(4, n)

        @pl.when(turns)
        def _():
            move(4, 5, n, 5, p_ys).start()

        relay_side(n)

    def back(src, kind, h, to):
        return pltpu.make_async_remote_copy(
            src_ref=part.at[src, h],
            dst_ref=rin.at[kind, h],
            send_sem=back_send.at[src, h],
            recv_sem=back_recv.at[kind, h],
            device_id=to,
            device_id_type=MESH,
        )

    def joined(src, kind, h):
        for c in range(2):
            both = part[src, h, c].astype(F32) + rin[kind, h, c].astype(F32)
            part[src, h, c] = both.astype(BF16)

    def back_first(h):
        back(2, 0, h, p_ym2).start()

        @pl.when(jnp.logical_not(turns))
        def _():
            back(0, 3, h, p_y1).start()

    def back_second(h):
        back(2, 0, h, p_ym2).wait_recv()
        joined(1, 0, h)

        @pl.when(turns)
        def _():
            back(1, 1, h, p_ys).start()

        @pl.when(jnp.logical_not(turns))
        def _():
            back(1, 2, h, p_y2).start()

    def back_third(h):
        @pl.when(turns)
        def _():
            back(1, 1, h, p_ys).wait_recv()
            joined(0, 1, h)
            back(0, 3, h, p_y1).start()

    def back_last(h):
        back(0, 3, h, p_y1).wait_recv()
        dk[h] += rin[3, h, 0].astype(F32)
        dv[h] += rin[3, h, 1].astype(F32)

        @pl.when(turns)
        def _():
            back(1, 2, h, p_y2).wait_recv()
            dk[h] += rin[2, h, 0].astype(F32)
            dv[h] += rin[2, h, 1].astype(F32)

    def relay_far(n):
        arrived(5, n)
        move(5, 6, n, 6, p_ym2).start()

    def z_move(phase, d):
        return pltpu.make_async_remote_copy(
            src_ref=zbuf.at[phase, 0],
            dst_ref=zbuf.at[phase, d],
            send_sem=z_send.at[phase, d],
            recv_sem=z_recv.at[phase, d],
            device_id=z_peers[d - 1],
            device_id_type=MESH,
        )

    def z_sum(phase):
        total = zbuf[phase, 0]
        for d in range(1, 8):
            z_move(phase, d).wait_recv()
            total = total + zbuf[phase, d]
        return total

    def small_move(buf, send, recv, band):
        return pltpu.make_async_remote_copy(
            src_ref=buf.at[0],
            dst_ref=buf.at[band],
            send_sem=send.at[band],
            recv_sem=recv.at[band],
            device_id=partners[band - 1],
            device_id_type=MESH,
        )

    fact_move = functools.partial(small_move, fact, fact_send, fact_recv)
    stat_move = functools.partial(small_move, stat, stat_send, stat_recv)

    for n in range(WINDOW):
        load(n).wait()
        send_own(n)
    for n in range(WINDOW, 12):
        load(n).wait()

    ones = jnp.ones((8, HD), F32)

    query_sq = jnp.zeros((8, 2 * TILE), F32)
    key_sq = jnp.zeros((8, 2 * TILE), F32)
    for h in range(heads):
        q_vals = slab[0, 6 + 2 * h].astype(F32)
        k_vals = slab[0, 2 * h].astype(F32)
        query_sq += dot_nt(ones, q_vals * q_vals, lax.Precision.HIGHEST)
        key_sq += dot_nt(ones, k_vals * k_vals, lax.Precision.HIGHEST)
    zbuf[0, 0, 0:1, :] = query_sq[0:1]
    zbuf[0, 0, 1:2, :] = key_sq[0:1]
    for d in range(1, 8):
        z_move(0, d).start()
    def gain_of(h):
        cols = pl.ds(h * HD, HD)
        return (query_gain[cols] * key_gain[cols] * scale)[None, :]

    def factors():
        fact[0] = lax.rsqrt(z_sum(0) / width + EPS)
        for band in range(1, BANDS):
            fact_move(band).start()
        colq[...] = columns_of(fact[0, 0:1, :])
        colk[...] = columns_of(fact[0, 1:2, :])
        for h in range(heads):
            both = gain_of(h) * LOG2E
            qt[h] = (slab[0, 6 + 2 * h].astype(F32) * colq[...] * both).astype(BF16)
            kt[h] = (slab[0, 2 * h].astype(F32) * colk[...] * both).astype(BF16)

    def shift_of(b, h, r, c):
        return jnp.where(mask[r, c, b] > 0, bias[h, b] * LOG2E, NEG)

    halves = [slice(0, TILE), slice(TILE, 2 * TILE)]

    def score_bands(h, low, high):
        def body(b, carry):
            factor = fact[b, 1:2, :]
            for r in range(2):
                scores = dot_nt(qt[h, halves[r], :], slab[b, 2 * h])
                top = mrun[halves[r], :]
                for c in range(2):
                    part = scores[:, halves[c]] * factor[:, halves[c]] + shift_of(b, h, r, c)
                    sbuf[b, halves[r], halves[c]] = part
                    top = jnp.maximum(top, part)
                mrun[halves[r], :] = top
            return carry

        lax.fori_loop(low, high, body, 0, unroll=True)

    def forward(h):
        top = jnp.max(mrun[...], axis=1, keepdims=True)
        acc[...] = jnp.zeros_like(acc)

        def exp_band(b, carry):
            for r in range(2):
                total = acc[halves[r], :]
                for c in range(2):
                    e = jnp.exp2(sbuf[b, halves[r], halves[c]] - top[halves[r], :])
                    sbuf[b, halves[r], halves[c]] = e
                    total = total + e
                acc[halves[r], :] = total
            return carry

        lax.fori_loop(0, BANDS, exp_band, 0, unroll=True)
        total = jnp.sum(acc[...], axis=1, keepdims=True)
        inverse = 1.0 / total
        lse = top + jnp.log(total) * LOG2E
        acc[...] = jnp.zeros_like(acc)

        def out_band(b, carry):
            for r in range(2):
                p = (sbuf[b, halves[r], :] * inverse[halves[r], :]).astype(BF16)
                pbuf[b, halves[r], :] = p
                acc[halves[r], :] += dot_nn(p, slab[b, 2 * h + 1])
            return carry

        lax.fori_loop(0, BANDS, out_band, 0, unroll=True)
        att = acc[...].astype(BF16)
        stage[0, h] = att
        store(0, h).start()
        delta = jnp.sum(slab[0, 7 + 2 * h].astype(F32) * att.astype(F32), axis=1, keepdims=True)
        stat[0, h : h + 1, :] = jnp.broadcast_to(lse, (2 * TILE, TILE)).T[0:1, :]
        stat[0, 3 + h : 4 + h, :] = jnp.broadcast_to(delta, (2 * TILE, TILE)).T[0:1, :]
        dq[h] = jnp.zeros_like(acc)

        normed = (slab[0, 6 + 2 * h].astype(F32) * colq[...]).astype(BF16)

        def grad_band(b):
            factor = fact[b, 1:2, :]
            send_back = h < BACK and b >= 4
            for r in range(2):
                dp = dot_nt(slab[0, 7 + 2 * h, halves[r], :], slab[b, 2 * h + 1])
                p = pbuf[b, halves[r], :].astype(F32)
                ds = p * (dp - delta[halves[r], :])
                if send_back:
                    dsb[halves[r], :] = ds.astype(BF16)
                dq[h, halves[r], :] += dot_nn((ds * factor).astype(BF16), slab[b, 2 * h])
            if send_back:
                part[b - 4, h, 0] = dot_tn(dsb[...], normed).astype(BF16)
                part[b - 4, h, 1] = dot_tn(pbuf[b], slab[0, 7 + 2 * h]).astype(BF16)

        for b in reversed(range(BANDS)):
            grad_band(b)
            if h < BACK and b == 4:
                back_first(h)

    def key_bands(h, low, high):
        def body(b, carry):
            factor = fact[b, 0:1, :]
            lse = stat[b, h : h + 1, :]
            delta = stat[b, 3 + h : 4 + h, :]
            for r in range(2):
                scores = dot_nt(kt[h, halves[r], :], slab[b, 6 + 2 * h])
                parts = []
                for c in range(2):
                    rest = shift_of(b, h, r, c) - lse[:, halves[c]]
                    parts.append(jnp.exp2(scores[:, halves[c]] * factor[:, halves[c]] + rest))
                p = jnp.concatenate(parts, axis=1)
                dv[h, halves[r], :] += dot_nn(p.astype(BF16), slab[b, 7 + 2 * h])
                dp = dot_nt(slab[0, 2 * h + 1, halves[r], :], slab[b, 7 + 2 * h])
                ds = (p * (dp - delta) * factor).astype(BF16)
                dk[h, halves[r], :] += dot_nn(ds, slab[b, 6 + 2 * h])
            return carry

        lax.fori_loop(low, high, body, 0, unroll=True)

    outs = [att_out, dq_out, dk_out, dv_out]

    def store(which, h):
        return pltpu.make_async_copy(
            stage.at[which, h], outs[which].at[:, pl.ds(h * HD, HD)], store_sem.at[which, h]
        )

    def inner_add(phase, total, base, h):
        scaled = total[h] * gain_of(h)
        total[h] = scaled
        part = dot_nt(ones, scaled * slab[0, base + 2 * h].astype(F32), lax.Precision.HIGHEST)[0:1]
        if h > 0:
            part += zbuf[phase, 0, 0:1, :]
        zbuf[phase, 0, 0:1, :] = part[0:1]

    def inner_start(phase):
        for d in range(1, 8):
            z_move(phase, d).start()

    def inner_finish(phase, total, base, col, which):
        inner = columns_of(z_sum(phase)[0:1, :] / width)
        factor = col[...]
        cubed = factor * factor * factor * inner
        for h in range(heads):
            vals = slab[0, base + 2 * h].astype(F32)
            stage[which, h] = (factor * total[h] - vals * cubed).astype(BF16)
            store(which, h).start()

    dk[...] = jnp.zeros_like(dk)
    zbuf[1, 0] = jnp.zeros((2, 2 * TILE), F32)
    zbuf[2, 0] = jnp.zeros((2, 2 * TILE), F32)
    dv[...] = jnp.zeros_like(dv)

    def all_here(n):
        for k in (n, n + 1):
            arrived(1, k)
            arrived(3, k)
            arrived(6, k)

    def query_side(h):
        all_here(2 * h)
        mrun[...] = jnp.full(mrun.shape, NEG, F32)
        score_bands(h, 0, BANDS)
        forward(h)
        inner_add(1, dq, 6, h)

    sides = list(range(6, 6 + 2 * BACK))
    later = {}
    for h in range(BACK):
        later.setdefault(2 * h + 5, []).append(functools.partial(back_second, h))
        later.setdefault(2 * h + 7, []).append(functools.partial(back_third, h))
    for m in range(len(main)):
        if m > 0:
            relay_far(main[m - 1])
        relay(main[m])
        if m + WINDOW < len(main):
            send_own(main[m + WINDOW])
        if m > 2 and sides:
            relay_side(sides.pop(0))
        if 0 < m <= 2 * BACK:
            send_side(5 + m)
        if m == 1:
            factors()
        if m == 2:
            for band in range(1, BANDS):
                fact_move(band).wait_recv()
        for step in later.pop(m, []):
            step()
        if m in (3, 5, 7):
            query_side((m - 3) // 2)
        if m == 7:
            for band in range(1, BANDS):
                stat_move(band).start()
            inner_start(1)
        if m == 8:
            for h in range(heads):
                key_bands(h, 0, 1)
            inner_finish(1, dq, 6, colq, 1)
    assert not sides and not later
    for band in range(1, 4):
        stat_move(band).wait_recv()

    def near(h):
        for k in (6 + 2 * h, 7 + 2 * h):
            arrived(1, k)
            arrived(3, k)

    def key_done(h):
        inner_add(2, dk, 0, h)
        stage[3, h] = dv[h].astype(BF16)
        store(3, h).start()

    for h in range(BACK):
        near(h)
        key_bands(h, 1, 4)
    relay_far(main[-1])
    for h in range(BACK):
        back_last(h)
        key_done(h)
    for band in range(4, BANDS):
        stat_move(band).wait_recv()
    for h in range(BACK, heads):
        n = 6 + 2 * h
        near(h)
        key_bands(h, 1, 6)
        arrived(6, n)
        arrived(6, n + 1)
        key_bands(h, 6, 7)
        key_done(h)
    inner_start(2)
    inner_finish(2, dk, 0, colk, 2)

    for which in range(4):
        for h in range(heads):
            store(which, h).wait()
    for phase in range(3):
        for d in range(1, 8):
            z_move(phase, d).wait_send()
    for band in range(1, BANDS):
        fact_move(band).wait_send()
        stat_move(band).wait_send()

    def sent(way, count):
        pltpu.make_async_remote_copy(
            src_ref=slab.at[0, 0:count],
            dst_ref=slab.at[1, 0:count],
            send_sem=send_sem.at[way],
            recv_sem=recv_sem.at[1, 0],
            device_id=p_core,
            device_id_type=MESH,
        ).wait_send()

    for way in (0, 1, 2):
        sent(way, 12)
    for way in (3, 6):
        sent(way, len(main))

    @pl.when(turns)
    def _():
        sent(4, len(main))
        sent(5, len(main))

    for h in range(BACK):
        for src in range(3):
            back(src, 0, h, p_y1).wait_send()


def hand_over(*refs):
    held, in_sem, out_sem = refs[8:]
    here = [pltpu.make_async_copy(refs[i], held.at[i], in_sem.at[i]) for i in range(4)]
    away = [pltpu.make_async_copy(held.at[i], refs[4 + i], out_sem.at[i]) for i in range(4)]
    for copy in here:
        copy.start()
    for i in range(4):
        here[i].wait()
        away[i].start()
    for copy in away:
        copy.wait()


def on_device(query_proj, key_proj, value, out_grad, query_gain, key_gain, band_bias, tile_mask):
    rows, cols = query_proj.shape
    width = cols * lax.axis_size("head")
    hbm = pl.BlockSpec(memory_space=pl.ANY)
    vmem = pl.BlockSpec(memory_space=pltpu.VMEM)
    smem = pl.BlockSpec(memory_space=pltpu.SMEM)
    heads = cols // HD
    outs = pl.pallas_call(
        functools.partial(kernel, width),
        out_shape=[jax.ShapeDtypeStruct((rows, cols), BF16)] * 4,
        in_specs=[hbm] * 4 + [vmem] * 2 + [smem] * 2,
        out_specs=[hbm] * 4,
        scratch_shapes=[
            pltpu.VMEM((BANDS, 4 * heads, rows, HD), BF16),
            pltpu.VMEM((BANDS, 2, rows), F32),
            pltpu.VMEM((BANDS, 8, rows), F32),
            pltpu.VMEM((3, 8, 2, rows), F32),
            pltpu.VMEM((heads, rows, HD), BF16),
            pltpu.VMEM((heads, rows, HD), BF16),
            pltpu.VMEM((rows, TILE), F32),
            pltpu.VMEM((rows, TILE), F32),
            pltpu.VMEM((BANDS, rows, rows), F32),
            pltpu.VMEM((BANDS, rows, rows), BF16),
            pltpu.VMEM((rows, TILE), F32),
            pltpu.VMEM((rows, TILE), F32),
            pltpu.VMEM((heads, rows, HD), F32),
            pltpu.VMEM((heads, rows, HD), F32),
            pltpu.VMEM((heads, rows, HD), F32),
            pltpu.VMEM((4, heads, rows, HD), BF16),
            pltpu.VMEM((3, BACK, 2, rows, HD), BF16),
            pltpu.VMEM((4, BACK, 2, rows, HD), BF16),
            pltpu.VMEM((rows, rows), BF16),
            pltpu.SemaphoreType.DMA((4, BACK)),
            pltpu.SemaphoreType.DMA((4, BACK)),
            pltpu.SemaphoreType.DMA((4 * heads,)),
            pltpu.SemaphoreType.DMA((4, heads)),
            pltpu.SemaphoreType.DMA((7,)),
            pltpu.SemaphoreType.DMA((BANDS, 4 * heads)),
            pltpu.SemaphoreType.DMA((BANDS,)),
            pltpu.SemaphoreType.DMA((BANDS,)),
            pltpu.SemaphoreType.DMA((BANDS,)),
            pltpu.SemaphoreType.DMA((BANDS,)),
            pltpu.SemaphoreType.DMA((3, 8)),
            pltpu.SemaphoreType.DMA((3, 8)),
        ],
        compiler_params=pltpu.CompilerParams(
            collective_id=0, has_side_effects=True, vmem_limit_bytes=60 * 2**20
        ),
    )(
        query_proj,
        key_proj,
        value,
        out_grad,
        query_gain,
        key_gain,
        band_bias.T,
        tile_mask.transpose(0, 2, 1),
    )
    return pl.pallas_call(
        hand_over,
        out_shape=[jax.ShapeDtypeStruct((rows, cols), BF16)] * 4,
        in_specs=[hbm] * 4,
        out_specs=[hbm] * 4,
        scratch_shapes=[
            pltpu.VMEM((4, rows, cols), BF16),
            pltpu.SemaphoreType.DMA((4,)),
            pltpu.SemaphoreType.DMA((4,)),
        ],
        compiler_params=pltpu.CompilerParams(vmem_limit_bytes=60 * 2**20),
    )(*outs)


def solution(mesh):
    placed = (
        P("ctx", "head"),
        P("ctx", "head"),
        P("ctx", "head"),
        P("ctx", "head"),
        P("head"),
        P("head"),
        P(None, "head"),
        P("ctx", None, None),
    )
    return jax.shard_map(
        on_device,
        mesh=mesh,
        in_specs=placed,
        out_specs=(P("ctx", "head"), P("ctx", "head"), P("ctx", "head"), P("ctx", "head")),
        check_vma=False,
    )
```

```python
import functools
import math

import jax
import jax.numpy as jnp
from jax import lax
from jax.experimental import pallas as pl
from jax.experimental.pallas import tpu as pltpu
from jax.sharding import PartitionSpec as P

HD = 128
TILE = 128
BANDS = 7
WINDOW = 2
BACK = 1
EPS = 1e-06
NEG = -1e30
LOG2E = math.log2(math.e)
MESH = pl.DeviceIdType.MESH
F32 = jnp.float32
BF16 = jnp.bfloat16


def dot_nt(a, b, precision=None):
    return lax.dot_general(
        a, b, (((1,), (1,)), ((), ())), preferred_element_type=F32, precision=precision
    )


def dot_nn(a, b):
    return lax.dot_general(a, b, (((1,), (0,)), ((), ())), preferred_element_type=F32)


def dot_tn(a, b):
    return lax.dot_general(a, b, (((0,), (0,)), ((), ())), preferred_element_type=F32)


def columns_of(row, lanes=128):
    return jnp.broadcast_to(row, (lanes, row.shape[1])).T


def kernel(
    width,
    query_hbm,
    key_hbm,
    value_hbm,
    grad_hbm,
    query_gain,
    key_gain,
    bias,
    mask,
    att_out,
    dq_out,
    dk_out,
    dv_out,
    slab,
    fact,
    stat,
    zbuf,
    qt,
    kt,
    colq,
    colk,
    sbuf,
    pbuf,
    mrun,
    acc,
    dq,
    dk,
    dv,
    stage,
    part,
    rin,
    dsb,
    back_send,
    back_recv,
    load_sem,
    store_sem,
    send_sem,
    recv_sem,
    fact_send,
    fact_recv,
    stat_send,
    stat_recv,
    z_send,
    z_recv,
):
    heads = 3
    scale = HD**-0.5
    ctx = lax.axis_index("ctx")
    z = lax.axis_index("head")
    core = lax.rem(ctx, 2)
    x = lax.rem(ctx // 2, 4)
    y = ctx // 8
    tx = 1 - 2 * lax.rem(x, 2)
    t = 1 - 2 * lax.rem(y, 2)
    s = 1 - 2 * lax.rem(y // 2, 2)
    turns = s != t

    def dev(xn, yn, cn=core):
        return ((lax.rem(yn + 16, 8) * 4 + lax.rem(xn + 8, 4)) * 2 + cn, z)

    p_core = dev(x, y, 1 - core)
    p_x1 = dev(x + tx, y)
    p_xm = dev(x - tx, y)
    p_x2 = dev(x + 2, y)
    p_y1 = dev(x, y + t)
    p_ym = dev(x, y - t)
    p_ys = dev(x, y + s)
    p_y2 = dev(x, y + 2 * s)
    p_ym2 = dev(x, y - 2 * s)
    p_y4 = dev(x, y + 4)
    partners = [p_core, p_x1, p_x2, p_y1, p_y2, p_y4]
    z_peers = [(ctx, lax.rem(z + d, 8)) for d in range(1, 8)]

    hbm = [key_hbm, value_hbm, query_hbm, grad_hbm]

    def load(n):
        if n < 6:
            array, h = n % 2, n // 2
        else:
            array, h = 2 + n % 2, (n - 6) // 2
        return pltpu.make_async_copy(
            hbm[array].at[:, pl.ds(h * HD, HD)], slab.at[0, n], load_sem.at[n]
        )

    barrier = pltpu.get_barrier_semaphore()
    far_first = [z_peers[d - 1] for d in (4, 3, 5, 2, 6, 1, 7)]
    peers = far_first + [p_y4, p_y2, p_ym2, p_x2, p_y1, p_ym, p_x1, p_xm, p_core]
    for peer in peers:
        pl.semaphore_signal(barrier, inc=1, device_id=peer, device_id_type=MESH)
    for n in (0, 1, 6, 2, 8, 4, 10, 3, 5, 7, 9, 11):
        load(n).start()
    pl.semaphore_wait(barrier, len(peers))

    def move(src, dst, n, way, to):
        return pltpu.make_async_remote_copy(
            src_ref=slab.at[src, n],
            dst_ref=slab.at[dst, n],
            send_sem=send_sem.at[way],
            recv_sem=recv_sem.at[dst, n],
            device_id=to,
            device_id_type=MESH,
        )

    def arrived(dst, n):
        move(0, dst, n, 0, p_core).wait_recv()

    main = list(range(6)) + list(range(6 + 2 * BACK, 12))

    def send_side(n):
        move(0, 2, n, 1, p_x1).start()
        move(0, 1, n, 0, p_core).start()

    def send_own(n):
        move(0, 4, n, 3, p_y1).start()

        @pl.when(turns)
        def _():
            move(0, 5, n, 4, p_y2).start()

        send_side(n)

    def relay_side(n):
        arrived(2, n)
        move(2, 3, n, 2, p_xm).start()

    def relay(n):
        arrived(4, n)

        @pl.when(turns)
        def _():
            move(4, 5, n, 5, p_ys).start()

        relay_side(n)

    def back(src, kind, h, to):
        return pltpu.make_async_remote_copy(
            src_ref=part.at[src, h],
            dst_ref=rin.at[kind, h],
            send_sem=back_send.at[src, h],
            recv_sem=back_recv.at[kind, h],
            device_id=to,
            device_id_type=MESH,
        )

    def joined(src, kind, h):
        for c in range(2):
            both = part[src, h, c].astype(F32) + rin[kind, h, c].astype(F32)
            part[src, h, c] = both.astype(BF16)

    def back_first(h):
        back(2, 0, h, p_ym2).start()

        @pl.when(jnp.logical_not(turns))
        def _():
            back(0, 3, h, p_y1).start()

    def back_second(h):
        back(2, 0, h, p_ym2).wait_recv()
        joined(1, 0, h)

        @pl.when(turns)
        def _():
            back(1, 1, h, p_ys).start()

        @pl.when(jnp.logical_not(turns))
        def _():
            back(1, 2, h, p_y2).start()

    def back_third(h):
        @pl.when(turns)
        def _():
            back(1, 1, h, p_ys).wait_recv()
            joined(0, 1, h)
            back(0, 3, h, p_y1).start()

    def back_last(h):
        back(0, 3, h, p_y1).wait_recv()
        dk[h] += rin[3, h, 0].astype(F32)
        dv[h] += rin[3, h, 1].astype(F32)

        @pl.when(turns)
        def _():
            back(1, 2, h, p_y2).wait_recv()
            dk[h] += rin[2, h, 0].astype(F32)
            dv[h] += rin[2, h, 1].astype(F32)

    def relay_far(n):
        arrived(5, n)
        move(5, 6, n, 6, p_ym2).start()

    def z_move(phase, d):
        return pltpu.make_async_remote_copy(
            src_ref=zbuf.at[phase, 0],
            dst_ref=zbuf.at[phase, d],
            send_sem=z_send.at[phase, d],
            recv_sem=z_recv.at[phase, d],
            device_id=z_peers[d - 1],
            device_id_type=MESH,
        )

    def z_sum(phase):
        total = zbuf[phase, 0]
        for d in range(1, 8):
            z_move(phase, d).wait_recv()
            total = total + zbuf[phase, d]
        return total

    def small_move(buf, send, recv, band):
        return pltpu.make_async_remote_copy(
            src_ref=buf.at[0],
            dst_ref=buf.at[band],
            send_sem=send.at[band],
            recv_sem=recv.at[band],
            device_id=partners[band - 1],
            device_id_type=MESH,
        )

    fact_move = functools.partial(small_move, fact, fact_send, fact_recv)
    stat_move = functools.partial(small_move, stat, stat_send, stat_recv)

    for n in range(WINDOW):
        load(n).wait()
        send_own(n)
    for n in range(WINDOW, 12):
        load(n).wait()

    ones = jnp.ones((8, HD), F32)

    query_sq = jnp.zeros((8, 2 * TILE), F32)
    key_sq = jnp.zeros((8, 2 * TILE), F32)
    for h in range(heads):
        q_vals = slab[0, 6 + 2 * h].astype(F32)
        k_vals = slab[0, 2 * h].astype(F32)
        query_sq += dot_nt(ones, q_vals * q_vals, lax.Precision.HIGHEST)
        key_sq += dot_nt(ones, k_vals * k_vals, lax.Precision.HIGHEST)
    zbuf[0, 0, 0:1, :] = query_sq[0:1]
    zbuf[0, 0, 1:2, :] = key_sq[0:1]
    for d in range(1, 8):
        z_move(0, d).start()
    def gain_of(h):
        cols = pl.ds(h * HD, HD)
        return (query_gain[cols] * key_gain[cols] * scale)[None, :]

    def factors():
        fact[0] = lax.rsqrt(z_sum(0) / width + EPS)
        for band in range(1, BANDS):
            fact_move(band).start()
        colq[...] = columns_of(fact[0, 0:1, :])
        colk[...] = columns_of(fact[0, 1:2, :])
        for h in range(heads):
            both = gain_of(h) * LOG2E
            qt[h] = (slab[0, 6 + 2 * h].astype(F32) * colq[...] * both).astype(BF16)
            kt[h] = (slab[0, 2 * h].astype(F32) * colk[...] * both).astype(BF16)

    def shift_of(b, h, r, c):
        return jnp.where(mask[r, c, b] > 0, bias[h, b] * LOG2E, NEG)

    halves = [slice(0, TILE), slice(TILE, 2 * TILE)]

    def score_bands(h, low, high):
        def body(b, carry):
            factor = fact[b, 1:2, :]
            for r in range(2):
                scores = dot_nt(qt[h, halves[r], :], slab[b, 2 * h])
                top = mrun[halves[r], :]
                for c in range(2):
                    part = scores[:, halves[c]] * factor[:, halves[c]] + shift_of(b, h, r, c)
                    sbuf[b, halves[r], halves[c]] = part
                    top = jnp.maximum(top, part)
                mrun[halves[r], :] = top
            return carry

        lax.fori_loop(low, high, body, 0, unroll=True)

    def forward(h):
        top = jnp.max(mrun[...], axis=1, keepdims=True)
        acc[...] = jnp.zeros_like(acc)

        def exp_band(b, carry):
            for r in range(2):
                total = acc[halves[r], :]
                for c in range(2):
                    e = jnp.exp2(sbuf[b, halves[r], halves[c]] - top[halves[r], :])
                    sbuf[b, halves[r], halves[c]] = e
                    total = total + e
                acc[halves[r], :] = total
            return carry

        lax.fori_loop(0, BANDS, exp_band, 0, unroll=True)
        total = jnp.sum(acc[...], axis=1, keepdims=True)
        inverse = 1.0 / total
        lse = top + jnp.log(total) * LOG2E
        acc[...] = jnp.zeros_like(acc)

        def out_band(b, carry):
            for r in range(2):
                p = (sbuf[b, halves[r], :] * inverse[halves[r], :]).astype(BF16)
                pbuf[b, halves[r], :] = p
                acc[halves[r], :] += dot_nn(p, slab[b, 2 * h + 1])
            return carry

        lax.fori_loop(0, BANDS, out_band, 0, unroll=True)
        att = acc[...].astype(BF16)
        stage[0, h] = att
        store(0, h).start()
        delta = jnp.sum(slab[0, 7 + 2 * h].astype(F32) * att.astype(F32), axis=1, keepdims=True)
        stat[0, h : h + 1, :] = jnp.broadcast_to(lse, (2 * TILE, TILE)).T[0:1, :]
        stat[0, 3 + h : 4 + h, :] = jnp.broadcast_to(delta, (2 * TILE, TILE)).T[0:1, :]
        dq[h] = jnp.zeros_like(acc)

        normed = (slab[0, 6 + 2 * h].astype(F32) * colq[...]).astype(BF16)

        def grad_band(b):
            factor = fact[b, 1:2, :]
            send_back = h < BACK and b >= 4
            for r in range(2):
                dp = dot_nt(slab[0, 7 + 2 * h, halves[r], :], slab[b, 2 * h + 1])
                p = pbuf[b, halves[r], :].astype(F32)
                ds = p * (dp - delta[halves[r], :])
                if send_back:
                    dsb[halves[r], :] = ds.astype(BF16)
                dq[h, halves[r], :] += dot_nn((ds * factor).astype(BF16), slab[b, 2 * h])
            if send_back:
                part[b - 4, h, 0] = dot_tn(dsb[...], normed).astype(BF16)
                part[b - 4, h, 1] = dot_tn(pbuf[b], slab[0, 7 + 2 * h]).astype(BF16)

        for b in reversed(range(BANDS)):
            grad_band(b)
            if h < BACK and b == 4:
                back_first(h)

    def key_bands(h, low, high):
        def body(b, carry):
            factor = fact[b, 0:1, :]
            lse = stat[b, h : h + 1, :]
            delta = stat[b, 3 + h : 4 + h, :]
            for r in range(2):
                scores = dot_nt(kt[h, halves[r], :], slab[b, 6 + 2 * h])
                parts = []
                for c in range(2):
                    rest = shift_of(b, h, r, c) - lse[:, halves[c]]
                    parts.append(jnp.exp2(scores[:, halves[c]] * factor[:, halves[c]] + rest))
                p = jnp.concatenate(parts, axis=1)
                dv[h, halves[r], :] += dot_nn(p.astype(BF16), slab[b, 7 + 2 * h])
                dp = dot_nt(slab[0, 2 * h + 1, halves[r], :], slab[b, 7 + 2 * h])
                ds = (p * (dp - delta) * factor).astype(BF16)
                dk[h, halves[r], :] += dot_nn(ds, slab[b, 6 + 2 * h])
            return carry

        lax.fori_loop(low, high, body, 0, unroll=True)

    outs = [att_out, dq_out, dk_out, dv_out]

    def store(which, h):
        return pltpu.make_async_copy(
            stage.at[which, h], outs[which].at[:, pl.ds(h * HD, HD)], store_sem.at[which, h]
        )

    def inner_add(phase, total, base, h):
        scaled = total[h] * gain_of(h)
        total[h] = scaled
        part = dot_nt(ones, scaled * slab[0, base + 2 * h].astype(F32), lax.Precision.HIGHEST)[0:1]
        if h > 0:
            part += zbuf[phase, 0, 0:1, :]
        zbuf[phase, 0, 0:1, :] = part[0:1]

    def inner_start(phase):
        for d in (4, 3, 5, 2, 6, 1, 7):
            z_move(phase, d).start()

    def inner_finish(phase, total, base, col, which):
        inner = columns_of(z_sum(phase)[0:1, :] / width)
        factor = col[...]
        cubed = factor * factor * factor * inner
        for h in range(heads):
            vals = slab[0, base + 2 * h].astype(F32)
            stage[which, h] = (factor * total[h] - vals * cubed).astype(BF16)
            store(which, h).start()

    dk[...] = jnp.zeros_like(dk)
    zbuf[1, 0] = jnp.zeros((2, 2 * TILE), F32)
    zbuf[2, 0] = jnp.zeros((2, 2 * TILE), F32)
    dv[...] = jnp.zeros_like(dv)

    def all_here(n):
        for k in (n, n + 1):
            arrived(1, k)
            arrived(3, k)
            arrived(6, k)

    def query_side(h):
        all_here(2 * h)
        mrun[...] = jnp.full(mrun.shape, NEG, F32)
        score_bands(h, 0, BANDS)
        forward(h)
        inner_add(1, dq, 6, h)

    sides = list(range(6, 6 + 2 * BACK))
    later = {}
    for h in range(BACK):
        later.setdefault(2 * h + 5, []).append(functools.partial(back_second, h))
        later.setdefault(2 * h + 7, []).append(functools.partial(back_third, h))
    for m in range(len(main)):
        if m > 0:
            relay_far(main[m - 1])
        relay(main[m])
        if m + WINDOW < len(main):
            send_own(main[m + WINDOW])
        if m > 2 and sides:
            relay_side(sides.pop(0))
        if 0 < m <= 2 * BACK:
            send_side(5 + m)
        if m == 1:
            factors()
        if m == 2:
            for band in range(1, BANDS):
                fact_move(band).wait_recv()
        for step in later.pop(m, []):
            step()
        if m in (3, 5, 7):
            query_side((m - 3) // 2)
        if m == 7:
            for band in range(1, BANDS):
                stat_move(band).start()
            inner_start(1)
        if m == 8:
            for h in range(heads):
                key_bands(h, 0, 1)
            inner_finish(1, dq, 6, colq, 1)
    assert not sides and not later
    for band in range(1, 4):
        stat_move(band).wait_recv()

    def near(h):
        for k in (6 + 2 * h, 7 + 2 * h):
            arrived(1, k)
            arrived(3, k)

    def key_done(h):
        inner_add(2, dk, 0, h)
        stage[3, h] = dv[h].astype(BF16)
        store(3, h).start()

    for h in range(BACK):
        near(h)
        key_bands(h, 1, 4)
    relay_far(main[-1])
    for h in range(BACK):
        back_last(h)
        key_done(h)
    for band in range(4, BANDS):
        stat_move(band).wait_recv()
    for h in range(BACK, heads):
        n = 6 + 2 * h
        near(h)
        key_bands(h, 1, 6)
        arrived(6, n)
        arrived(6, n + 1)
        key_bands(h, 6, 7)
        key_done(h)
    inner_start(2)
    inner_finish(2, dk, 0, colk, 2)

    for which in range(4):
        for h in range(heads):
            store(which, h).wait()
    for phase in range(3):
        for d in range(1, 8):
            z_move(phase, d).wait_send()
    for band in range(1, BANDS):
        fact_move(band).wait_send()
        stat_move(band).wait_send()

    def sent(way, count):
        pltpu.make_async_remote_copy(
            src_ref=slab.at[0, 0:count],
            dst_ref=slab.at[1, 0:count],
            send_sem=send_sem.at[way],
            recv_sem=recv_sem.at[1, 0],
            device_id=p_core,
            device_id_type=MESH,
        ).wait_send()

    for way in (0, 1, 2):
        sent(way, 12)
    for way in (3, 6):
        sent(way, len(main))

    @pl.when(turns)
    def _():
        sent(4, len(main))
        sent(5, len(main))

    for h in range(BACK):
        for src in range(3):
            back(src, 0, h, p_y1).wait_send()


def hand_over(*refs):
    held, in_sem, out_sem = refs[8:]
    here = [pltpu.make_async_copy(refs[i], held.at[i], in_sem.at[i]) for i in range(4)]
    away = [pltpu.make_async_copy(held.at[i], refs[4 + i], out_sem.at[i]) for i in range(4)]
    for copy in here:
        copy.start()
    for i in range(4):
        here[i].wait()
        away[i].start()
    for copy in away:
        copy.wait()


def on_device(query_proj, key_proj, value, out_grad, query_gain, key_gain, band_bias, tile_mask):
    rows, cols = query_proj.shape
    width = cols * lax.axis_size("head")
    hbm = pl.BlockSpec(memory_space=pl.ANY)
    vmem = pl.BlockSpec(memory_space=pltpu.VMEM)
    smem = pl.BlockSpec(memory_space=pltpu.SMEM)
    heads = cols // HD
    outs = pl.pallas_call(
        functools.partial(kernel, width),
        out_shape=[jax.ShapeDtypeStruct((rows, cols), BF16)] * 4,
        in_specs=[hbm] * 4 + [vmem] * 2 + [smem] * 2,
        out_specs=[hbm] * 4,
        scratch_shapes=[
            pltpu.VMEM((BANDS, 4 * heads, rows, HD), BF16),
            pltpu.VMEM((BANDS, 2, rows), F32),
            pltpu.VMEM((BANDS, 8, rows), F32),
            pltpu.VMEM((3, 8, 2, rows), F32),
            pltpu.VMEM((heads, rows, HD), BF16),
            pltpu.VMEM((heads, rows, HD), BF16),
            pltpu.VMEM((rows, TILE), F32),
            pltpu.VMEM((rows, TILE), F32),
            pltpu.VMEM((BANDS, rows, rows), F32),
            pltpu.VMEM((BANDS, rows, rows), BF16),
            pltpu.VMEM((rows, TILE), F32),
            pltpu.VMEM((rows, TILE), F32),
            pltpu.VMEM((heads, rows, HD), F32),
            pltpu.VMEM((heads, rows, HD), F32),
            pltpu.VMEM((heads, rows, HD), F32),
            pltpu.VMEM((4, heads, rows, HD), BF16),
            pltpu.VMEM((3, BACK, 2, rows, HD), BF16),
            pltpu.VMEM((4, BACK, 2, rows, HD), BF16),
            pltpu.VMEM((rows, rows), BF16),
            pltpu.SemaphoreType.DMA((4, BACK)),
            pltpu.SemaphoreType.DMA((4, BACK)),
            pltpu.SemaphoreType.DMA((4 * heads,)),
            pltpu.SemaphoreType.DMA((4, heads)),
            pltpu.SemaphoreType.DMA((7,)),
            pltpu.SemaphoreType.DMA((BANDS, 4 * heads)),
            pltpu.SemaphoreType.DMA((BANDS,)),
            pltpu.SemaphoreType.DMA((BANDS,)),
            pltpu.SemaphoreType.DMA((BANDS,)),
            pltpu.SemaphoreType.DMA((BANDS,)),
            pltpu.SemaphoreType.DMA((3, 8)),
            pltpu.SemaphoreType.DMA((3, 8)),
        ],
        compiler_params=pltpu.CompilerParams(
            collective_id=0, has_side_effects=True, vmem_limit_bytes=60 * 2**20
        ),
    )(
        query_proj,
        key_proj,
        value,
        out_grad,
        query_gain,
        key_gain,
        band_bias.T,
        tile_mask.transpose(0, 2, 1),
    )
    return pl.pallas_call(
        hand_over,
        out_shape=[jax.ShapeDtypeStruct((rows, cols), BF16)] * 4,
        in_specs=[hbm] * 4,
        out_specs=[hbm] * 4,
        scratch_shapes=[
            pltpu.VMEM((4, rows, cols), BF16),
            pltpu.SemaphoreType.DMA((4,)),
            pltpu.SemaphoreType.DMA((4,)),
        ],
        compiler_params=pltpu.CompilerParams(vmem_limit_bytes=60 * 2**20),
    )(*outs)


def solution(mesh):
    placed = (
        P("ctx", "head"),
        P("ctx", "head"),
        P("ctx", "head"),
        P("ctx", "head"),
        P("head"),
        P("head"),
        P(None, "head"),
        P("ctx", None, None),
    )
    return jax.shard_map(
        on_device,
        mesh=mesh,
        in_specs=placed,
        out_specs=(P("ctx", "head"), P("ctx", "head"), P("ctx", "head"), P("ctx", "head")),
        check_vma=False,
    )
```
